32 devices in a mesh: grp: 2 (over core), seq: 4 (over y, x), head: 4 (over z).
Axes of the slice: x: 2, y: 2, z: 4, core: 2. Of those that a mesh axis runs over, the one named last changes fastest.
Arguments:
- queries: bfloat16 [1024, 2048], P(('grp', 'seq'), 'head'), may hold values from -100 to 100
- keys: bfloat16 [2, 4096, 2048], P(None, ('grp', 'seq'), 'head'), may hold values from -15 to 15
- values: bfloat16 [2, 4096, 2048], P(None, ('grp', 'seq'), 'head'), may hold values from -6 to 6
- grad_out: bfloat16 [1024, 2048], P(('grp', 'seq', 'head')), may hold values from -6 to 6
- pad_counts: int32 [2], replicated, may hold values from 0 to 256, as said below
Outputs:
- context: bfloat16 [1024, 2048], P(('grp', 'seq', 'head'))
- grad_queries: bfloat16 [1024, 2048], P(('grp', 'seq'), 'head')
- grad_keys: bfloat16 [2, 4096, 2048], P(None, ('grp', 'seq'), 'head')
- grad_values: bfloat16 [2, 4096, 2048], P(None, ('grp', 'seq'), 'head')
The draws below stay inside these ranges and needn't reach their ends.
Inputs may be any that keep to these rules, and one draw needn't show every extreme that they name: `pad_counts`: each count is at most 256, and in every draw one pair has exactly 256 padding tokens.
All inputs are finite; a program needn't handle non-finite values.
Results may differ from the reference program's by a relative error of at most 0.0215.
Values may be sent and summed in bfloat16 or wider, within the bound.
No kernel may reach another device: no remote copies, remote signals or barrier semaphores. Data moves between devices by JAX's collectives and lax.ppermute only.
A program may use at most 64 MiB of HBM per device.

```python
import math
import jax
import jax.numpy as jnp
from jax import lax

HEADS = 32
HEAD_DIM = 64
BATCH = 2
TGT = 512
SRC = 4096


def key_table(key):
    rows = jax.random.normal(jax.random.fold_in(key, 5), (BATCH, SRC, HEADS * HEAD_DIM), jnp.float32) * 2.5
    rows = jnp.clip(rows, -15.0, 15.0)
    return rows


def draw_keys(key, part):
    return key_table(key).astype(jnp.bfloat16)


def draw_queries(key, part):
    key = jax.random.fold_in(key, 7)
    total_rows = BATCH * TGT
    width = HEADS * HEAD_DIM
    base = jnp.clip(jax.random.normal(key, (total_rows, width), jnp.float32), -6.0, 6.0)
    spread = 12.0
    loud = jax.random.randint(jax.random.fold_in(key, 1), (total_rows, 1), 0, 4, jnp.int32) == 0
    strong = jnp.clip(jax.random.normal(jax.random.fold_in(key, 2), (total_rows, width), jnp.float32) * spread, -100.0, 100.0)
    base = jnp.where(loud, strong, base)
    return base.astype(jnp.bfloat16)


def draw_pad_counts(key, part):
    key = jax.random.fold_in(key, 9)
    most = TGT // 2
    counts = jax.random.randint(key, (BATCH,), 0, most + 1, jnp.int32)
    first = jax.random.randint(jax.random.fold_in(key, 1), (), 0, BATCH, jnp.int32)
    index = jnp.arange(BATCH, dtype=jnp.int32)
    return jnp.where(index == first, most, counts)


def shard_levels(stream_key, dims, split, low, high):
    level = 1.0
    for dim, parts in split:
        draws = jax.random.uniform(jax.random.fold_in(jax.random.fold_in(stream_key, 6), dim), (parts,), jnp.float32, low / len(split), high / len(split))
        level = level * jnp.repeat(jnp.exp(draws), dims[dim] // parts).reshape((-1,) + (1,) * (len(dims) - 1 - dim))
    return level


def scatter_about(stream_key, extent, scale, reach, pieces=(), held_as=jnp.bfloat16):
    gain = shard_levels(stream_key, extent, pieces, -0.22, 0.18) if pieces else 1.0
    values = jax.random.normal(stream_key, extent, jnp.float32) * scale * gain
    return jnp.minimum(jnp.maximum(values, -reach), reach).astype(held_as)


def setup_inputs(seed: int = 0) -> dict:
    arg_keys = jax.random.split(jax.random.key(seed), 6)
    queries = draw_queries(jax.random.fold_in(arg_keys[5], 71), 0)
    keys = draw_keys(jax.random.fold_in(arg_keys[5], 71), 0)
    values = scatter_about(arg_keys[2], (BATCH, SRC, HEADS * HEAD_DIM), 1.0, 6.0, ((1, 8), (2, 4)))
    grad_out = scatter_about(arg_keys[3], (BATCH * TGT, HEADS * HEAD_DIM), 1.0, 6.0, ((0, 32),))
    pad_counts = draw_pad_counts(jax.random.fold_in(arg_keys[5], 71), 0)
    return dict(queries=queries, keys=keys, values=values, grad_out=grad_out, pad_counts=pad_counts)


def reference(queries, keys, values, grad_out, pad_counts):
    scale = 1.0 / math.sqrt(HEAD_DIM)
    width = HEADS * HEAD_DIM
    position = jnp.arange(TGT, dtype=jnp.int32)
    block = math.gcd(TGT, 64)
    count = TGT // block
    contexts = []
    query_grads = []
    key_grads = []
    value_grads = []
    for pair in range(BATCH):
        valid = (position < TGT - pad_counts[pair]).astype(jnp.float32)
        key_rows = keys[pair].astype(jnp.float32).reshape(SRC, HEADS, HEAD_DIM)
        value_rows = values[pair].astype(jnp.float32).reshape(SRC, HEADS, HEAD_DIM)
        query_blocks = queries[pair * TGT:(pair + 1) * TGT].reshape(count, block, HEADS, HEAD_DIM)
        grad_blocks = grad_out[pair * TGT:(pair + 1) * TGT].reshape(count, block, HEADS, HEAD_DIM)
        valid_blocks = valid.reshape(count, block)

        def step(carry, item):
            grad_k, grad_v = carry
            query, grad, mask = item
            query = query.astype(jnp.float32)
            scores = jnp.einsum('thd,phd->htp', query, key_rows) * scale
            top = lax.optimization_barrier(jnp.max(scores, axis=-1, keepdims=True))
            expo = jnp.exp(scores - top)
            probs = expo / lax.optimization_barrier(jnp.sum(expo, axis=-1, keepdims=True))
            weights = lax.optimization_barrier(probs.astype(jnp.bfloat16)).astype(jnp.float32)
            attended = jnp.einsum('htp,phd->thd', weights, value_rows) * mask[:, None, None]
            masked = grad.astype(jnp.float32) * mask[:, None, None]
            delta = lax.optimization_barrier(jnp.sum(masked * attended, axis=-1)).T
            grad_probs = jnp.einsum('thd,phd->htp', masked, value_rows)
            grad_scores = (probs * (grad_probs - delta[:, :, None]) * scale).astype(jnp.bfloat16)
            grad_scores = lax.optimization_barrier(grad_scores).astype(jnp.float32)
            grad_q = jnp.einsum('htp,phd->thd', grad_scores, key_rows)
            grad_k = grad_k + jnp.einsum('htp,thd->phd', grad_scores, query)
            grad_v = grad_v + jnp.einsum('htp,thd->phd', weights, masked)
            return ((grad_k, grad_v), (attended.astype(jnp.bfloat16), grad_q.astype(jnp.bfloat16)))
        start = (jnp.zeros((SRC, HEADS, HEAD_DIM), jnp.float32), jnp.zeros((SRC, HEADS, HEAD_DIM), jnp.float32))
        (grad_k, grad_v), (context, grad_q) = lax.scan(step, start, (query_blocks, grad_blocks, valid_blocks))
        contexts.append(context.reshape(TGT, width))
        query_grads.append(grad_q.reshape(TGT, width))
        key_grads.append(grad_k.reshape(SRC, width).astype(jnp.bfloat16))
        value_grads.append(grad_v.reshape(SRC, width).astype(jnp.bfloat16))
    return (jnp.concatenate(contexts, axis=0), jnp.concatenate(query_grads, axis=0), jnp.stack(key_grads, axis=0), jnp.stack(value_grads, axis=0))
```

```python
import math

import jax
import jax.numpy as jnp
from jax import lax
from jax.experimental import pallas as pl
from jax.experimental.pallas import tpu as pltpu
from jax.sharding import PartitionSpec as P

HEAD_DIM = 64
PAIR = 128
LOG2E = math.log2(math.e)
F32 = jnp.float32
BF16 = jnp.bfloat16
VMEM_LIMIT = 28 * 1024 * 1024

NT = (((1,), (1,)), ((), ()))
NN = (((1,), (0,)), ((), ()))


def dot(a, b, dims):
    return lax.dot_general(a, b, dims, preferred_element_type=F32)


def lane_mask(head, value):
    lane = lax.broadcasted_iota(jnp.int32, (1, PAIR), 1)
    return jnp.where((lane // HEAD_DIM) == head, value, 0.0).astype(BF16)


def lane_scale():
    return jnp.full((1, PAIR), 1.0 / math.sqrt(HEAD_DIM), F32).astype(BF16)


def stack_slots(refs, slots, lanes):
    return jnp.concatenate([refs[k][:, lanes] for k in slots], axis=0)


def slot_valid(info, n, rows, k):
    valid = rows * n - info[2 + info[0]]
    return jnp.clip(valid - (info[1] ^ k) * rows, 0, rows)


def any_valid(info, n, rows, slots):
    return sum(slot_valid(info, n, rows, k) for k in slots) > 0


def target_blocks(n, rows):
    per = max(1, min(n, 256 // rows))
    return [list(range(first, min(first + per, n))) for first in range(0, n, per)]


def for_valid_blocks(n, rows, info, run):
    blocks = target_blocks(n, rows)
    some = [any_valid(info, n, rows, slots) for slots in blocks]
    for case in range(1, 1 << len(blocks)):
        chosen = [b for b in range(len(blocks)) if case >> b & 1]
        wanted = True
        for b in range(len(blocks)):
            wanted = jnp.logical_and(wanted, some[b] if b in chosen else jnp.logical_not(some[b]))

        @pl.when(wanted)
        def _(chosen=chosen):
            rest = [blocks[b] for b in range(len(blocks)) if b not in chosen]
            run([blocks[b] for b in chosen], rest)


def chunked(refs):
    rows = min(256, refs[0].shape[0])
    return [x[i * rows : (i + 1) * rows] for x in refs for i in range(x.shape[0] // rows)]


def head_rows(x, u):
    zero = jnp.zeros((HEAD_DIM, x.shape[1]), BF16)
    part = x[u * HEAD_DIM : (u + 1) * HEAD_DIM]
    return jnp.concatenate([part, zero] if u == 0 else [zero, part], axis=0)


def minus_rows(x):
    high = x.astype(BF16).astype(F32)
    mid = (x - high).astype(BF16).astype(F32)
    low = x - high - mid
    row = lax.broadcasted_iota(jnp.int32, (16, x.shape[1]), 0)
    top = jnp.where(row == 0, -high, jnp.where(row == 1, -mid, jnp.where(row == 2, -low, 0.0))).astype(BF16)
    return jnp.concatenate([top, jnp.zeros((PAIR - 16, x.shape[1]), BF16)], axis=0)


def with_ones(x):
    lane = lax.broadcasted_iota(jnp.int32, (x.shape[0], PAIR), 1)
    return jnp.concatenate([x, (lane < 3).astype(F32).astype(BF16)], axis=1)


def forward_kernel(n, rows, info, *refs):
    q = refs[:n]
    k_own, v_own, k_oth, v_oth, lse_ref, top_ref, out_ref, exp_ref = refs[n:]
    first_pair = pl.program_id(0) * lse_ref.shape[0]

    def run(blocks, rest):
        def sources(own, oth, lanes):
            return chunked([own[0, :, lanes], oth[0, :, lanes]])

        ks, vts, qts = {}, {}, {}
        for p in range(lse_ref.shape[0]):
            lanes = slice(p * PAIR, (p + 1) * PAIR)
            ks[p] = sources(k_own, k_oth, lanes)
            vt = [x.T for x in sources(v_own, v_oth, lanes)]
            row = lax.broadcasted_iota(jnp.int32, (16, vt[0].shape[1]), 0)
            ones = (row == 0).astype(F32).astype(BF16)
            for u in range(2):
                vts[p, u] = [jnp.concatenate([x[u * HEAD_DIM : (u + 1) * HEAD_DIM], ones], axis=0) for x in vt]
            for b, slots in enumerate(blocks):
                qts[p, b] = (stack_slots(q, slots, lanes) * lane_scale()).T

        def scores(chain):
            p, b, u = chain
            qm = head_rows(qts[p, b], u)
            s = [dot(k, qm, NN) for k in ks[p]]
            top = jnp.max(s[0], axis=0, keepdims=True)
            for x in s[1:]:
                top = jnp.maximum(top, jnp.max(x, axis=0, keepdims=True))
            return s, top

        def output(chain, s, top):
            p, b, u = chain
            o = None
            block = target_blocks(n, rows).index(blocks[b])
            for c, (x, v) in enumerate(zip(s, vts[p, u])):
                e = jnp.exp2((x - top) * LOG2E).astype(BF16)
                exp_ref[first_pair + p, 2 * block + u, c] = e
                part = dot(v, e, NN)
                o = part if o is None else o + part
            total = o[HEAD_DIM : HEAD_DIM + 1]
            cols = pl.ds(blocks[b][0] * rows, rows * len(blocks[b]))
            lse_ref[p, u : u + 1, cols] = top + jnp.log(total)
            top_ref[p, u : u + 1, cols] = top
            out_ref[p * PAIR + u * HEAD_DIM : p * PAIR + (u + 1) * HEAD_DIM, cols] = o[:HEAD_DIM] / total

        chains = [(p, b, u) for p in range(lse_ref.shape[0]) for b in range(len(blocks)) for u in range(2)]
        ahead = scores(chains[0])
        for i, chain in enumerate(chains):
            now = ahead
            if i + 1 < len(chains):
                ahead = scores(chains[i + 1])
            output(chain, *now)
        for slots in rest:
            width = rows * len(slots)
            cols = pl.ds(slots[0] * rows, width)
            lse_ref[:, :, cols] = jnp.zeros((lse_ref.shape[0], 2, width), F32)
            top_ref[:, :, cols] = jnp.zeros((lse_ref.shape[0], 2, width), F32)
            out_ref[:, cols] = jnp.zeros((out_ref.shape[0], width), F32)

    for_valid_blocks(n, rows, info, run)


def slot_cotangents(g, info, n, slots, cols=slice(None)):
    blocks = []
    for k in slots:
        block = g[k][:, cols]
        row = lax.broadcasted_iota(jnp.int32, block.shape, 0)
        blocks.append(block * (row < slot_valid(info, n, block.shape[0], k)).astype(F32).astype(BF16))
    return jnp.concatenate(blocks, axis=0)


def delta_kernel(n, rows, info, *refs):
    g, (lse_ref, out_ref, stats_ref), sends = refs[:n], refs[n : n + 3], refs[n + 3 :]
    pairs = lse_ref.shape[0]
    for h in range(pairs):
        do = slot_cotangents(g, info, n, range(n), slice(h * PAIR, (h + 1) * PAIR)).T.astype(F32)
        prod = do * out_ref[h * PAIR : (h + 1) * PAIR]
        stats_ref[h, 0:2] = lse_ref[h]
        for u in range(2):
            part = prod[u * HEAD_DIM : (u + 1) * HEAD_DIM]
            stats_ref[h, 2 + u : 3 + u] = jnp.sum(part, axis=0, keepdims=True)
    for k in range(n):
        sends[k][...] = out_ref[:, k * rows : (k + 1) * rows].astype(BF16)


def merge(lses, deltas):
    top = lses[0]
    for x in lses[1:]:
        top = jnp.maximum(top, x)
    weights = [jnp.exp(x - top) for x in lses]
    total = sum(weights)
    delta = sum(w * d for w, d in zip(weights, deltas)) / total
    return top + jnp.log(total), delta


def backward_kernel(n, rows, info, *refs):
    q, g, stats = refs[:n], refs[n : 2 * n], refs[2 * n : 3 * n]
    k_own, v_own, k_oth, v_oth, top_ref, exp_ref = refs[3 * n : 3 * n + 6]
    dk_own, dv_own, d_oth = refs[3 * n + 6 : 3 * n + 9]
    dq = refs[3 * n + 9 :]
    first_pair = pl.program_id(0) * top_ref.shape[0]
    scale = 1.0 / math.sqrt(HEAD_DIM)

    def ordered(j, p, kind, u, slots):
        line = stats[j][p, 2 * kind + u : 2 * kind + u + 1]
        if rows % 128:
            return line[:, slots[0] * rows : (slots[-1] + 1) * rows]
        return jnp.concatenate([line[:, (k ^ j) * rows : ((k ^ j) + 1) * rows] for k in slots], axis=1)

    def run(blocks, rest):
        def sources(own, oth, lanes):
            return chunked([own[0, :, lanes], oth[0, :, lanes]])

        vs, kt, operands = {}, {}, {}
        pairs = stats[0].shape[0]
        for p in range(pairs):
            lanes = slice(p * PAIR, (p + 1) * PAIR)
            vs[p] = [with_ones(x) for x in sources(v_own, v_oth, lanes)]
            kt[p] = [x.T for x in sources(k_own, k_oth, lanes)]
            for b, slots in enumerate(blocks):
                qb = stack_slots(q, slots, lanes) * lane_scale()
                gb = slot_cotangents(g, info, n, slots, lanes)
                gt = gb.T
                cols = slice(slots[0] * rows, (slots[-1] + 1) * rows)
                for u in range(2):
                    lse, delta = merge(
                        [ordered(j, p, 0, u, slots) for j in range(n)], [ordered(j, p, 1, u, slots) for j in range(n)]
                    )
                    operands[p, b, u] = (
                        jnp.exp(top_ref[p, u : u + 1, cols] - lse),
                        jnp.concatenate([head_rows(gt, u), minus_rows(delta)], axis=0),
                        qb * lane_mask(u, 1.0),
                        gb * lane_mask(u, 1.0),
                    )
        count, size = len(vs[0]), vs[0][0].shape[0]
        dks, dvs, dqs = {}, {}, {}

        def add(sums, key, new):
            sums[key] = sums[key] + new if key in sums else new

        def first(item):
            chain, c = item
            return dot(vs[chain[0]][c], operands[chain][1], NN)

        def second(item, dp):
            chain, c = item
            p, b, u = chain
            weight, _, qm, gm = operands[chain]
            block = target_blocks(n, rows).index(blocks[b])
            prob = exp_ref[first_pair + p, 2 * block + u, c].astype(F32) * weight
            ds = (prob * dp).astype(BF16)
            add(dvs, (p, c), dot(prob.astype(BF16), gm, NN))
            add(dks, (p, c), dot(ds, qm, NN))
            add(dqs, chain, dot(kt[p][c][u * HEAD_DIM : (u + 1) * HEAD_DIM], ds, NN))

        def store(p):
            lanes = slice(p * PAIR, (p + 1) * PAIR)
            half = count // 2
            for c in range(half):
                at = slice(c * size, (c + 1) * size)
                dk_own[0, at, lanes] = dks[p, c].astype(BF16)
                dv_own[0, at, lanes] = dvs[p, c].astype(BF16)
                d_oth[0, at, lanes] = dks[p, half + c].astype(BF16)
                d_oth[1, at, lanes] = dvs[p, half + c].astype(BF16)

        chains = [(p, b, u) for p in range(pairs) for b in range(len(blocks)) for u in range(2)]
        items = [(chain, c) for chain in chains for c in range(count)]
        ahead = first(items[0])
        for i, item in enumerate(items):
            now = ahead
            if i + 1 < len(items):
                ahead = first(items[i + 1])
            second(item, now)
            chain, c = item
            if c == count - 1:
                p, b, u = chain
                total = dqs[chain] * scale
                feat = slice(p * PAIR + u * HEAD_DIM, p * PAIR + (u + 1) * HEAD_DIM)
                for j, k in enumerate(blocks[b]):
                    dq[k][feat] = total[:, j * rows : (j + 1) * rows].astype(BF16)
                if i + 1 == len(items) or items[i + 1][0][0] != p:
                    store(p)
        for slots in rest:
            for k in slots:
                dq[k][...] = jnp.zeros_like(dq[k])

    for_valid_blocks(n, rows, info, run)


def context_kernel(n, rows, info, *refs):
    outs, stats, context = refs[:n], refs[n : 2 * n], refs[2 * n]
    lane = lax.broadcasted_iota(jnp.int32, (1, rows), 1)
    valid = (lane < slot_valid(info, n, rows, 0)).astype(F32)
    heads = outs[0].shape[0] // HEAD_DIM
    parts = []
    for head in range(heads):
        feat = slice(head * HEAD_DIM, (head + 1) * HEAD_DIM)
        lses = []
        for j in range(n):
            slot = 0 if rows % 128 else j
            lses.append(stats[j][head // 2, head % 2 : head % 2 + 1, slot * rows : (slot + 1) * rows])
        top = lses[0]
        for x in lses[1:]:
            top = jnp.maximum(top, x)
        weights = [jnp.exp(x - top) for x in lses]
        keep = valid / sum(weights)
        parts.append(sum(outs[j][feat].astype(F32) * (weights[j] * keep) for j in range(n)))
    context[...] = jnp.concatenate(parts, axis=0).T.astype(BF16)


def split_kernel(grad, pieces):
    width = pieces.shape[2]
    for k in range(pieces.shape[0]):
        pieces[k] = grad[:, k * width : (k + 1) * width]


def fill_kernel(info, back, dk_in, dv_in, dk, dv):
    dk[0] = back[0]
    dv[0] = back[1]


def finish_kernel(n, *refs):
    dq, pieces, out, context = refs[:n], refs[n], refs[n + 1], refs[n + 2]
    total = dq[0][...].astype(F32)
    for ref in dq[1:]:
        total = total + ref[...].astype(F32)
    out[...] = total.T.astype(BF16)
    width = pieces.shape[2]
    for k in range(pieces.shape[0]):
        context[:, k * width : (k + 1) * width] = pieces[k]


def compiler_params():
    return pltpu.CompilerParams(vmem_limit_bytes=VMEM_LIMIT)


def stay(x):
    return pltpu.with_memory_space_constraint(x, pltpu.HBM)


def xor_permute(x, axis, size, k):
    return lax.ppermute(x, axis, [(i, i ^ k) for i in range(size)])


def local(queries, keys, values, grad_out, pad_counts):
    rows, width = queries.shape
    src = keys.shape[1]
    n, m = lax.axis_size("seq"), lax.axis_size("head")
    group, seq = lax.axis_index("grp"), lax.axis_index("seq")
    sub = rows // m
    tgt = rows * n
    pairs = width // PAIR
    step = 2 if pairs % 2 == 0 else 1
    sds = jax.ShapeDtypeStruct
    whole = pl.BlockSpec(memory_space=pltpu.VMEM)
    smem = pl.BlockSpec(memory_space=pltpu.SMEM)
    anywhere = pl.BlockSpec(memory_space=pl.ANY)

    info = jnp.concatenate([group[None], seq[None], pad_counts]).astype(jnp.int32)

    def gather(x):
        return [x] + [xor_permute(x, "seq", n, k) for k in range(1, n)]

    def exchange(x):
        return lax.all_to_all(x, "head", split_axis=0, concat_axis=0, tiled=True)

    def plain(kernel, in_specs, out_shape, *args):
        out_specs = jax.tree.map(lambda x: whole, out_shape)
        return pl.pallas_call(
            kernel, in_specs=in_specs, out_specs=out_specs, out_shape=out_shape, compiler_params=compiler_params()
        )(*args)

    def call(kernel, in_specs, out_specs, out_shape, args, flops=0, alias={}):
        return pl.pallas_call(
            kernel,
            grid_spec=pltpu.PrefetchScalarGridSpec(
                num_scalar_prefetch=1, grid=(pairs // step,), in_specs=in_specs, out_specs=out_specs
            ),
            out_shape=out_shape,
            input_output_aliases=alias,
            compiler_params=compiler_params(),
            cost_estimate=pl.CostEstimate(flops=flops, bytes_accessed=1 << 20, transcendentals=0),
        )(info, *args)

    lanes = step * PAIR
    slot_in = [pl.BlockSpec((rows, lanes), lambda h, info: (0, h))] * n
    slot_t = [pl.BlockSpec((lanes, rows), lambda h, info: (h, 0))] * n
    own = pl.BlockSpec((1, src, lanes), lambda h, info: (info[0], 0, h))
    away = pl.BlockSpec((1, src, lanes), lambda h, info: (1 - info[0], 0, h))
    oth = pl.BlockSpec((2, src, lanes), lambda h, info: (0, 0, h))
    lse_spec = pl.BlockSpec((step, 2, tgt), lambda h, info: (h, 0, 0))
    out_spec = pl.BlockSpec((lanes, tgt), lambda h, info: (h, 0))
    stats_spec = pl.BlockSpec((step, 4, tgt), lambda h, info: (h, 0, 0))

    q = gather(queries)
    k_oth, v_oth = xor_permute(keys, "grp", 2, 1), xor_permute(values, "grp", 2, 1)
    pieces = plain(split_kernel, [whole], sds((m, sub, width), BF16), stay(grad_out))
    g = gather(exchange(pieces).reshape(rows, width))

    flop = 24 * tgt * 2 * src * width
    chunk, per = min(256, src), rows * len(target_blocks(n, rows)[0])
    exps = (pairs, 2 * (tgt // per), 2 * src // chunk, chunk, per)
    lse, top, out_t, exps = call(
        lambda *a: forward_kernel(n, rows, *a),
        slot_in + [own] * 4,
        [lse_spec, lse_spec, out_spec, whole],
        [sds((pairs, 2, tgt), F32)] * 2 + [sds((width, tgt), F32), sds(exps, BF16)],
        [stay(queries), *q[1:], stay(keys), stay(values), k_oth, v_oth],
        flops=2 * flop,
    )
    stats, *sends = plain(
        lambda *a: delta_kernel(n, rows, *a),
        [smem] + [whole] * (n + 2),
        [sds((pairs, 4, tgt), F32)] + [sds((width, rows), BF16)] * n,
        info, *g, lse, out_t,
    )
    all_stats = gather(stats)
    if rows % 128:

        def reorder(x, j):
            return x.reshape(pairs, 4, n, rows)[:, :, [k ^ j for k in range(n)]].reshape(pairs, 4, tgt)

        all_stats = [all_stats[0]] + [reorder(all_stats[j], j) for j in range(1, n)]
    outs = [sends[0]] + [xor_permute(sends[k], "seq", n, k) for k in range(1, n)]
    grads = call(
        lambda *a: backward_kernel(n, rows, *a),
        slot_in + slot_in + [stats_spec] * n + [own] * 4 + [lse_spec, whole],
        [own, own, oth] + slot_t,
        [sds((2, src, width), BF16)] * 3 + [sds((width, rows), BF16)] * n,
        [stay(queries), *q[1:], *g, *all_stats, stay(keys), stay(values), k_oth, v_oth, top, exps],
        flops=4 * flop,
    )
    (dk, dv, d_oth, *dq), outs = lax.optimization_barrier((grads, outs))
    dq = [dq[0]] + [xor_permute(dq[k], "seq", n, k) for k in range(1, n)]
    back = xor_permute(d_oth, "grp", 2, 1)

    context = plain(
        lambda *a: context_kernel(n, rows, *a),
        [smem] + [whole] * (2 * n),
        sds((rows, width), BF16),
        info, *outs, *all_stats,
    )
    pieces = exchange(context.reshape(m, sub, width))
    grad_keys, grad_values = call(
        fill_kernel,
        [oth, anywhere, anywhere],
        [away] * 2,
        [sds((2, src, width), BF16)] * 2,
        [back, dk, dv],
        alias={2: 0, 3: 1},
    )
    dq, grad_keys, grad_values = lax.optimization_barrier((dq, grad_keys, grad_values))
    grad_queries, context = plain(
        lambda *a: finish_kernel(n, *a),
        [whole] * (n + 1),
        [sds((rows, width), BF16), sds((sub, m * width), BF16)],
        *dq, pieces,
    )
    return (context, grad_queries, grad_keys, grad_values)


def solution(mesh):
    return jax.shard_map(
        local,
        mesh=mesh,
        in_specs=(
            P(("grp", "seq"), "head"),
            P(None, ("grp", "seq"), "head"),
            P(None, ("grp", "seq"), "head"),
            P(("grp", "seq", "head"), None),
            P(),
        ),
        out_specs=(
            P(("grp", "seq", "head"), None),
            P(("grp", "seq"), "head"),
            P(None, ("grp", "seq"), "head"),
            P(None, ("grp", "seq"), "head"),
        ),
        check_vma=False,
    )
```

```python
import math

import jax
import jax.numpy as jnp
from jax import lax
from jax.experimental import pallas as pl
from jax.experimental.pallas import tpu as pltpu
from jax.sharding import PartitionSpec as P

HEAD_DIM = 64
PAIR = 128
LOG2E = math.log2(math.e)
F32 = jnp.float32
BF16 = jnp.bfloat16
VMEM_LIMIT = 16 * 1024 * 1024

NT = (((1,), (1,)), ((), ()))
NN = (((1,), (0,)), ((), ()))


def dot(a, b, dims):
    return lax.dot_general(a, b, dims, preferred_element_type=F32)


def lane_mask(head, value):
    lane = lax.broadcasted_iota(jnp.int32, (1, PAIR), 1)
    return jnp.where((lane // HEAD_DIM) == head, value, 0.0).astype(BF16)


def lane_scale():
    return jnp.full((1, PAIR), 1.0 / math.sqrt(HEAD_DIM), F32).astype(BF16)


def stack_slots(refs, slots, lanes):
    return jnp.concatenate([refs[k][:, lanes] for k in slots], axis=0)


def slot_valid(info, n, rows, k):
    valid = rows * n - info[2 + info[0]]
    return jnp.clip(valid - (info[1] ^ k) * rows, 0, rows)


def any_valid(info, n, rows, slots):
    return sum(slot_valid(info, n, rows, k) for k in slots) > 0


def target_blocks(n, rows):
    per = max(1, min(n, 256 // rows))
    return [list(range(first, min(first + per, n))) for first in range(0, n, per)]


def for_valid_blocks(n, rows, info, run):
    blocks = target_blocks(n, rows)
    some = [any_valid(info, n, rows, slots) for slots in blocks]
    for case in range(1, 1 << len(blocks)):
        chosen = [b for b in range(len(blocks)) if case >> b & 1]
        wanted = True
        for b in range(len(blocks)):
            wanted = jnp.logical_and(wanted, some[b] if b in chosen else jnp.logical_not(some[b]))

        @pl.when(wanted)
        def _(chosen=chosen):
            rest = [blocks[b] for b in range(len(blocks)) if b not in chosen]
            run([blocks[b] for b in chosen], rest)


def chunked(refs):
    rows = min(256, refs[0].shape[0])
    return [x[i * rows : (i + 1) * rows] for x in refs for i in range(x.shape[0] // rows)]


def head_rows(x, u):
    zero = jnp.zeros((HEAD_DIM, x.shape[1]), BF16)
    part = x[u * HEAD_DIM : (u + 1) * HEAD_DIM]
    return jnp.concatenate([part, zero] if u == 0 else [zero, part], axis=0)


def minus_rows(x):
    high = x.astype(BF16).astype(F32)
    mid = (x - high).astype(BF16).astype(F32)
    low = x - high - mid
    row = lax.broadcasted_iota(jnp.int32, (16, x.shape[1]), 0)
    top = jnp.where(row == 0, -high, jnp.where(row == 1, -mid, jnp.where(row == 2, -low, 0.0))).astype(BF16)
    return jnp.concatenate([top, jnp.zeros((PAIR - 16, x.shape[1]), BF16)], axis=0)


def with_ones(x):
    lane = lax.broadcasted_iota(jnp.int32, (x.shape[0], PAIR), 1)
    return jnp.concatenate([x, (lane < 3).astype(F32).astype(BF16)], axis=1)


def forward_kernel(n, rows, info, *refs):
    q = refs[:n]
    k_own, v_own, k_oth, v_oth, lse_ref, top_ref, out_ref, exp_ref = refs[n:]
    first_pair = pl.program_id(0) * lse_ref.shape[0]

    def run(blocks, rest):
        def sources(own, oth, lanes):
            return chunked([own[0, :, lanes], oth[0, :, lanes]])

        ks, vts, qts = {}, {}, {}
        for p in range(lse_ref.shape[0]):
            lanes = slice(p * PAIR, (p + 1) * PAIR)
            ks[p] = sources(k_own, k_oth, lanes)
            vt = [x.T for x in sources(v_own, v_oth, lanes)]
            row = lax.broadcasted_iota(jnp.int32, (16, vt[0].shape[1]), 0)
            ones = (row == 0).astype(F32).astype(BF16)
            for u in range(2):
                vts[p, u] = [jnp.concatenate([x[u * HEAD_DIM : (u + 1) * HEAD_DIM], ones], axis=0) for x in vt]
            for b, slots in enumerate(blocks):
                qts[p, b] = (stack_slots(q, slots, lanes) * lane_scale()).T

        def scores(chain):
            p, b, u = chain
            qm = head_rows(qts[p, b], u)
            s = [dot(k, qm, NN) for k in ks[p]]
            top = jnp.max(s[0], axis=0, keepdims=True)
            for x in s[1:]:
                top = jnp.maximum(top, jnp.max(x, axis=0, keepdims=True))
            return s, top

        def output(chain, s, top):
            p, b, u = chain
            o = None
            block = target_blocks(n, rows).index(blocks[b])
            for c, (x, v) in enumerate(zip(s, vts[p, u])):
                e = jnp.exp2((x - top) * LOG2E).astype(BF16)
                exp_ref[first_pair + p, 2 * block + u, c] = e
                part = dot(v, e, NN)
                o = part if o is None else o + part
            total = o[HEAD_DIM : HEAD_DIM + 1]
            cols = pl.ds(blocks[b][0] * rows, rows * len(blocks[b]))
            lse_ref[p, u : u + 1, cols] = top + jnp.log(total)
            top_ref[p, u : u + 1, cols] = top
            out_ref[p * PAIR + u * HEAD_DIM : p * PAIR + (u + 1) * HEAD_DIM, cols] = o[:HEAD_DIM] / total

        chains = [(p, b, u) for p in range(lse_ref.shape[0]) for b in range(len(blocks)) for u in range(2)]
        ahead = scores(chains[0])
        for i, chain in enumerate(chains):
            now = ahead
            if i + 1 < len(chains):
                ahead = scores(chains[i + 1])
            output(chain, *now)
        for slots in rest:
            width = rows * len(slots)
            cols = pl.ds(slots[0] * rows, width)
            lse_ref[:, :, cols] = jnp.zeros((lse_ref.shape[0], 2, width), F32)
            top_ref[:, :, cols] = jnp.zeros((lse_ref.shape[0], 2, width), F32)
            out_ref[:, cols] = jnp.zeros((out_ref.shape[0], width), F32)

    for_valid_blocks(n, rows, info, run)


def slot_cotangents(g, info, n, slots, cols=slice(None)):
    blocks = []
    for k in slots:
        block = g[k][:, cols]
        row = lax.broadcasted_iota(jnp.int32, block.shape, 0)
        blocks.append(block * (row < slot_valid(info, n, block.shape[0], k)).astype(F32).astype(BF16))
    return jnp.concatenate(blocks, axis=0)


def delta_kernel(n, rows, info, *refs):
    g, (lse_ref, out_ref, stats_ref), sends = refs[:n], refs[n : n + 3], refs[n + 3 :]
    pairs = lse_ref.shape[0]
    for h in range(pairs):
        do = slot_cotangents(g, info, n, range(n), slice(h * PAIR, (h + 1) * PAIR)).T.astype(F32)
        prod = do * out_ref[h * PAIR : (h + 1) * PAIR]
        stats_ref[h, 0:2] = lse_ref[h]
        for u in range(2):
            part = prod[u * HEAD_DIM : (u + 1) * HEAD_DIM]
            stats_ref[h, 2 + u : 3 + u] = jnp.sum(part, axis=0, keepdims=True)
    for k in range(n):
        sends[k][...] = out_ref[:, k * rows : (k + 1) * rows].astype(BF16)


def merge(lses, deltas):
    top = lses[0]
    for x in lses[1:]:
        top = jnp.maximum(top, x)
    weights = [jnp.exp(x - top) for x in lses]
    total = sum(weights)
    delta = sum(w * d for w, d in zip(weights, deltas)) / total
    return top + jnp.log(total), delta


def backward_kernel(n, rows, info, *refs):
    q, g, stats = refs[:n], refs[n : 2 * n], refs[2 * n : 3 * n]
    k_own, v_own, k_oth, v_oth, top_ref, exp_ref = refs[3 * n : 3 * n + 6]
    dk_own, dv_own, d_oth = refs[3 * n + 6 : 3 * n + 9]
    dq = refs[3 * n + 9 :]
    first_pair = pl.program_id(0) * top_ref.shape[0]
    scale = 1.0 / math.sqrt(HEAD_DIM)

    def ordered(j, p, kind, u, slots):
        line = stats[j][p, 2 * kind + u : 2 * kind + u + 1]
        if rows % 128:
            return line[:, slots[0] * rows : (slots[-1] + 1) * rows]
        return jnp.concatenate([line[:, (k ^ j) * rows : ((k ^ j) + 1) * rows] for k in slots], axis=1)

    def run(blocks, rest):
        def sources(own, oth, lanes):
            return chunked([own[0, :, lanes], oth[0, :, lanes]])

        vs, kt, operands = {}, {}, {}
        pairs = stats[0].shape[0]
        for p in range(pairs):
            lanes = slice(p * PAIR, (p + 1) * PAIR)
            vs[p] = [with_ones(x) for x in sources(v_own, v_oth, lanes)]
            kt[p] = [x.T for x in sources(k_own, k_oth, lanes)]
            for b, slots in enumerate(blocks):
                qb = stack_slots(q, slots, lanes) * lane_scale()
                gb = slot_cotangents(g, info, n, slots, lanes)
                gt = gb.T
                cols = slice(slots[0] * rows, (slots[-1] + 1) * rows)
                for u in range(2):
                    lse, delta = merge(
                        [ordered(j, p, 0, u, slots) for j in range(n)], [ordered(j, p, 1, u, slots) for j in range(n)]
                    )
                    operands[p, b, u] = (
                        jnp.exp(top_ref[p, u : u + 1, cols] - lse),
                        jnp.concatenate([head_rows(gt, u), minus_rows(delta)], axis=0),
                        qb * lane_mask(u, 1.0),
                        gb * lane_mask(u, 1.0),
                    )
        count, size = len(vs[0]), vs[0][0].shape[0]
        dks, dvs, dqs = {}, {}, {}

        def add(sums, key, new):
            sums[key] = sums[key] + new if key in sums else new

        def first(item):
            chain, c = item
            return dot(vs[chain[0]][c], operands[chain][1], NN)

        def second(item, dp):
            chain, c = item
            p, b, u = chain
            weight, _, qm, gm = operands[chain]
            block = target_blocks(n, rows).index(blocks[b])
            prob = exp_ref[first_pair + p, 2 * block + u, c].astype(F32) * weight
            ds = (prob * dp).astype(BF16)
            add(dvs, (p, c), dot(prob.astype(BF16), gm, NN))
            add(dks, (p, c), dot(ds, qm, NN))
            add(dqs, chain, dot(kt[p][c][u * HEAD_DIM : (u + 1) * HEAD_DIM], ds, NN))

        def store(p):
            lanes = slice(p * PAIR, (p + 1) * PAIR)
            half = count // 2
            for c in range(half):
                at = slice(c * size, (c + 1) * size)
                dk_own[0, at, lanes] = dks[p, c].astype(BF16)
                dv_own[0, at, lanes] = dvs[p, c].astype(BF16)
                d_oth[0, at, lanes] = dks[p, half + c].astype(BF16)
                d_oth[1, at, lanes] = dvs[p, half + c].astype(BF16)

        chains = [(p, b, u) for p in range(pairs) for b in range(len(blocks)) for u in range(2)]
        items = [(chain, c) for chain in chains for c in range(count)]
        ahead = first(items[0])
        for i, item in enumerate(items):
            now = ahead
            if i + 1 < len(items):
                ahead = first(items[i + 1])
            second(item, now)
            chain, c = item
            if c == count - 1:
                p, b, u = chain
                total = dqs[chain] * scale
                feat = slice(p * PAIR + u * HEAD_DIM, p * PAIR + (u + 1) * HEAD_DIM)
                for j, k in enumerate(blocks[b]):
                    dq[k][feat] = total[:, j * rows : (j + 1) * rows].astype(BF16)
                if i + 1 == len(items) or items[i + 1][0][0] != p:
                    store(p)
        for slots in rest:
            for k in slots:
                dq[k][...] = jnp.zeros_like(dq[k])

    for_valid_blocks(n, rows, info, run)


def context_kernel(n, rows, info, *refs):
    outs, stats, context = refs[:n], refs[n : 2 * n], refs[2 * n]
    lane = lax.broadcasted_iota(jnp.int32, (1, rows), 1)
    valid = (lane < slot_valid(info, n, rows, 0)).astype(F32)
    heads = outs[0].shape[0] // HEAD_DIM
    parts = []
    for head in range(heads):
        feat = slice(head * HEAD_DIM, (head + 1) * HEAD_DIM)
        lses = []
        for j in range(n):
            slot = 0 if rows % 128 else j
            lses.append(stats[j][head // 2, head % 2 : head % 2 + 1, slot * rows : (slot + 1) * rows])
        top = lses[0]
        for x in lses[1:]:
            top = jnp.maximum(top, x)
        weights = [jnp.exp(x - top) for x in lses]
        keep = valid / sum(weights)
        parts.append(sum(outs[j][feat].astype(F32) * (weights[j] * keep) for j in range(n)))
    context[...] = jnp.concatenate(parts, axis=0).T.astype(BF16)


def split_kernel(grad, pieces, sems):
    width = pieces.shape[2]
    copies = [
        pltpu.make_async_copy(grad.at[:, k * width : (k + 1) * width], pieces.at[k], sems.at[k])
        for k in range(pieces.shape[0])
    ]
    for c in copies:
        c.start()
    for c in copies:
        c.wait()


def fill_kernel(info, back, dk_in, dv_in, dk, dv):
    dk[0] = back[0]
    dv[0] = back[1]


def finish_kernel(n, *refs):
    dq, pieces, out, context = refs[:n], refs[n], refs[n + 1], refs[n + 2]
    total = dq[0][...].astype(F32)
    for ref in dq[1:]:
        total = total + ref[...].astype(F32)
    out[...] = total.T.astype(BF16)
    width = pieces.shape[2]
    for k in range(pieces.shape[0]):
        context[:, k * width : (k + 1) * width] = pieces[k]


def compiler_params():
    return pltpu.CompilerParams(vmem_limit_bytes=VMEM_LIMIT)


def stay(x):
    return pltpu.with_memory_space_constraint(x, pltpu.HBM)


def xor_permute(x, axis, size, k):
    return lax.ppermute(x, axis, [(i, i ^ k) for i in range(size)])


def local(queries, keys, values, grad_out, pad_counts):
    rows, width = queries.shape
    src = keys.shape[1]
    n, m = lax.axis_size("seq"), lax.axis_size("head")
    group, seq = lax.axis_index("grp"), lax.axis_index("seq")
    sub = rows // m
    tgt = rows * n
    pairs = width // PAIR
    step = 2 if pairs % 2 == 0 else 1
    sds = jax.ShapeDtypeStruct
    whole = pl.BlockSpec(memory_space=pltpu.VMEM)
    smem = pl.BlockSpec(memory_space=pltpu.SMEM)
    anywhere = pl.BlockSpec(memory_space=pl.ANY)

    info = jnp.concatenate([group[None], seq[None], pad_counts]).astype(jnp.int32)

    def gather(x):
        return [x] + [xor_permute(x, "seq", n, k) for k in range(1, n)]

    def exchange(x):
        return lax.all_to_all(x, "head", split_axis=0, concat_axis=0, tiled=True)

    def plain(kernel, in_specs, out_shape, *args):
        out_specs = jax.tree.map(lambda x: whole, out_shape)
        return pl.pallas_call(
            kernel, in_specs=in_specs, out_specs=out_specs, out_shape=out_shape, compiler_params=compiler_params()
        )(*args)

    def call(kernel, in_specs, out_specs, out_shape, args, flops=0, alias={}):
        return pl.pallas_call(
            kernel,
            grid_spec=pltpu.PrefetchScalarGridSpec(
                num_scalar_prefetch=1, grid=(pairs // step,), in_specs=in_specs, out_specs=out_specs
            ),
            out_shape=out_shape,
            input_output_aliases=alias,
            compiler_params=compiler_params(),
            cost_estimate=pl.CostEstimate(flops=flops, bytes_accessed=1 << 20, transcendentals=0),
        )(info, *args)

    lanes = step * PAIR
    slot_in = [pl.BlockSpec((rows, lanes), lambda h, info: (0, h))] * n
    slot_t = [pl.BlockSpec((lanes, rows), lambda h, info: (h, 0))] * n
    own = pl.BlockSpec((1, src, lanes), lambda h, info: (info[0], 0, h))
    away = pl.BlockSpec((1, src, lanes), lambda h, info: (1 - info[0], 0, h))
    oth = pl.BlockSpec((2, src, lanes), lambda h, info: (0, 0, h))
    lse_spec = pl.BlockSpec((step, 2, tgt), lambda h, info: (h, 0, 0))
    out_spec = pl.BlockSpec((lanes, tgt), lambda h, info: (h, 0))
    stats_spec = pl.BlockSpec((step, 4, tgt), lambda h, info: (h, 0, 0))

    q = gather(queries)
    k_oth, v_oth = xor_permute(keys, "grp", 2, 1), xor_permute(values, "grp", 2, 1)
    pieces = pl.pallas_call(
        split_kernel,
        in_specs=[pl.BlockSpec(memory_space=pltpu.HBM)],
        out_specs=whole,
        out_shape=sds((m, sub, width), BF16),
        scratch_shapes=[pltpu.SemaphoreType.DMA((m,))],
    )(stay(grad_out))
    g = gather(exchange(pieces).reshape(rows, width))

    flop = 24 * tgt * 2 * src * width
    chunk, per = min(256, src), rows * len(target_blocks(n, rows)[0])
    exps = (pairs, 2 * (tgt // per), 2 * src // chunk, chunk, per)
    lse, top, out_t, exps = call(
        lambda *a: forward_kernel(n, rows, *a),
        slot_in + [own] * 4,
        [lse_spec, lse_spec, out_spec, whole],
        [sds((pairs, 2, tgt), F32)] * 2 + [sds((width, tgt), F32), sds(exps, BF16)],
        [stay(queries), *q[1:], stay(keys), stay(values), k_oth, v_oth],
        flops=2 * flop,
    )
    stats, *sends = plain(
        lambda *a: delta_kernel(n, rows, *a),
        [smem] + [whole] * (n + 2),
        [sds((pairs, 4, tgt), F32)] + [sds((width, rows), BF16)] * n,
        info, *g, lse, out_t,
    )
    all_stats = gather(stats)
    if rows % 128:

        def reorder(x, j):
            return x.reshape(pairs, 4, n, rows)[:, :, [k ^ j for k in range(n)]].reshape(pairs, 4, tgt)

        all_stats = [all_stats[0]] + [reorder(all_stats[j], j) for j in range(1, n)]
    outs = [sends[0]] + [xor_permute(sends[k], "seq", n, k) for k in range(1, n)]
    grads = call(
        lambda *a: backward_kernel(n, rows, *a),
        slot_in + slot_in + [stats_spec] * n + [own] * 4 + [lse_spec, whole],
        [own, own, oth] + slot_t,
        [sds((2, src, width), BF16)] * 3 + [sds((width, rows), BF16)] * n,
        [stay(queries), *q[1:], *g, *all_stats, stay(keys), stay(values), k_oth, v_oth, top, exps],
        flops=4 * flop,
    )
    (dk, dv, d_oth, *dq), outs = lax.optimization_barrier((grads, outs))
    dq = [dq[0]] + [xor_permute(dq[k], "seq", n, k) for k in range(1, n)]
    back = xor_permute(d_oth, "grp", 2, 1)

    context = plain(
        lambda *a: context_kernel(n, rows, *a),
        [smem] + [whole] * (2 * n),
        sds((rows, width), BF16),
        info, *outs, *all_stats,
    )
    pieces = exchange(context.reshape(m, sub, width))
    grad_keys, grad_values = call(
        fill_kernel,
        [oth, anywhere, anywhere],
        [away] * 2,
        [sds((2, src, width), BF16)] * 2,
        [back, dk, dv],
        alias={2: 0, 3: 1},
    )
    dq, grad_keys, grad_values = lax.optimization_barrier((dq, grad_keys, grad_values))
    grad_queries, context = plain(
        lambda *a: finish_kernel(n, *a),
        [whole] * (n + 1),
        [sds((rows, width), BF16), sds((sub, m * width), BF16)],
        *dq, pieces,
    )
    return (context, grad_queries, grad_keys, grad_values)


def solution(mesh):
    return jax.shard_map(
        local,
        mesh=mesh,
        in_specs=(
            P(("grp", "seq"), "head"),
            P(None, ("grp", "seq"), "head"),
            P(None, ("grp", "seq"), "head"),
            P(("grp", "seq", "head"), None),
            P(),
        ),
        out_specs=(
            P(("grp", "seq", "head"), None),
            P(("grp", "seq"), "head"),
            P(None, ("grp", "seq"), "head"),
            P(None, ("grp", "seq"), "head"),
        ),
        check_vma=False,
    )
```

```python
import math

import jax
import jax.numpy as jnp
from jax import lax
from jax.experimental import pallas as pl
from jax.experimental.pallas import tpu as pltpu
from jax.sharding import PartitionSpec as P

HEAD_DIM = 64
PAIR = 128
LOG2E = math.log2(math.e)
F32 = jnp.float32
BF16 = jnp.bfloat16
VMEM_LIMIT = 16 * 1024 * 1024

NT = (((1,), (1,)), ((), ()))
NN = (((1,), (0,)), ((), ()))


def dot(a, b, dims):
    return lax.dot_general(a, b, dims, preferred_element_type=F32)


def lane_mask(head, value):
    lane = lax.broadcasted_iota(jnp.int32, (1, PAIR), 1)
    return jnp.where((lane // HEAD_DIM) == head, value, 0.0).astype(BF16)


def lane_scale():
    return jnp.full((1, PAIR), 1.0 / math.sqrt(HEAD_DIM), F32).astype(BF16)


def stack_slots(refs, slots, lanes):
    return jnp.concatenate([refs[k][:, lanes] for k in slots], axis=0)


def slot_valid(info, n, rows, k):
    valid = rows * n - info[2 + info[0]]
    return jnp.clip(valid - (info[1] ^ k) * rows, 0, rows)


def any_valid(info, n, rows, slots):
    return sum(slot_valid(info, n, rows, k) for k in slots) > 0


def target_blocks(n, rows):
    per = max(1, min(n, 256 // rows))
    return [list(range(first, min(first + per, n))) for first in range(0, n, per)]


def for_valid_blocks(n, rows, info, run):
    blocks = target_blocks(n, rows)
    some = [any_valid(info, n, rows, slots) for slots in blocks]
    for case in range(1, 1 << len(blocks)):
        chosen = [b for b in range(len(blocks)) if case >> b & 1]
        wanted = True
        for b in range(len(blocks)):
            wanted = jnp.logical_and(wanted, some[b] if b in chosen else jnp.logical_not(some[b]))

        @pl.when(wanted)
        def _(chosen=chosen):
            rest = [blocks[b] for b in range(len(blocks)) if b not in chosen]
            run([blocks[b] for b in chosen], rest)


def chunked(refs):
    rows = min(256, refs[0].shape[0])
    return [x[i * rows : (i + 1) * rows] for x in refs for i in range(x.shape[0] // rows)]


def head_rows(x, u):
    zero = jnp.zeros((HEAD_DIM, x.shape[1]), BF16)
    part = x[u * HEAD_DIM : (u + 1) * HEAD_DIM]
    return jnp.concatenate([part, zero] if u == 0 else [zero, part], axis=0)


def minus_rows(x):
    high = x.astype(BF16).astype(F32)
    mid = (x - high).astype(BF16).astype(F32)
    low = x - high - mid
    row = lax.broadcasted_iota(jnp.int32, (16, x.shape[1]), 0)
    top = jnp.where(row == 0, -high, jnp.where(row == 1, -mid, jnp.where(row == 2, -low, 0.0))).astype(BF16)
    return jnp.concatenate([top, jnp.zeros((PAIR - 16, x.shape[1]), BF16)], axis=0)


def with_ones(x):
    lane = lax.broadcasted_iota(jnp.int32, (x.shape[0], PAIR), 1)
    return jnp.concatenate([x, (lane < 3).astype(F32).astype(BF16)], axis=1)


def forward_kernel(n, rows, info, *refs):
    q = refs[:n]
    k_own, v_own, k_oth, v_oth, lse_ref, top_ref, out_ref, exp_ref, kt_ref, v_ref = refs[n:]
    first_pair = pl.program_id(0) * lse_ref.shape[0]

    def run(blocks, rest):
        def sources(own, oth, lanes):
            return chunked([own[0, :, lanes], oth[0, :, lanes]])

        ks, vts, qts = {}, {}, {}
        for p in range(lse_ref.shape[0]):
            lanes = slice(p * PAIR, (p + 1) * PAIR)
            ks[p] = sources(k_own, k_oth, lanes)
            vs = sources(v_own, v_oth, lanes)
            vt = [x.T for x in vs]
            for c in range(len(vs)):
                kt_ref[first_pair + p, c] = ks[p][c].T
                v_ref[first_pair + p, c] = vs[c]
            row = lax.broadcasted_iota(jnp.int32, (16, vt[0].shape[1]), 0)
            ones = (row == 0).astype(F32).astype(BF16)
            for u in range(2):
                vts[p, u] = [jnp.concatenate([x[u * HEAD_DIM : (u + 1) * HEAD_DIM], ones], axis=0) for x in vt]
            for b, slots in enumerate(blocks):
                qts[p, b] = (stack_slots(q, slots, lanes) * lane_scale()).T

        def scores(chain):
            p, b, u = chain
            qm = head_rows(qts[p, b], u)
            s = [dot(k, qm, NN) for k in ks[p]]
            top = jnp.max(s[0], axis=0, keepdims=True)
            for x in s[1:]:
                top = jnp.maximum(top, jnp.max(x, axis=0, keepdims=True))
            return s, top

        def output(chain, s, top):
            p, b, u = chain
            o = None
            block = target_blocks(n, rows).index(blocks[b])
            for c, (x, v) in enumerate(zip(s, vts[p, u])):
                e = jnp.exp2((x - top) * LOG2E).astype(BF16)
                exp_ref[first_pair + p, 2 * block + u, c] = e
                part = dot(v, e, NN)
                o = part if o is None else o + part
            total = o[HEAD_DIM : HEAD_DIM + 1]
            cols = pl.ds(blocks[b][0] * rows, rows * len(blocks[b]))
            lse_ref[p, u : u + 1, cols] = top + jnp.log(total)
            top_ref[p, u : u + 1, cols] = top
            out_ref[p * PAIR + u * HEAD_DIM : p * PAIR + (u + 1) * HEAD_DIM, cols] = o[:HEAD_DIM] / total

        chains = [(p, b, u) for p in range(lse_ref.shape[0]) for b in range(len(blocks)) for u in range(2)]
        ahead = scores(chains[0])
        for i, chain in enumerate(chains):
            now = ahead
            if i + 1 < len(chains):
                ahead = scores(chains[i + 1])
            output(chain, *now)
        for slots in rest:
            width = rows * len(slots)
            cols = pl.ds(slots[0] * rows, width)
            lse_ref[:, :, cols] = jnp.zeros((lse_ref.shape[0], 2, width), F32)
            top_ref[:, :, cols] = jnp.zeros((lse_ref.shape[0], 2, width), F32)
            out_ref[:, cols] = jnp.zeros((out_ref.shape[0], width), F32)

    for_valid_blocks(n, rows, info, run)


def slot_cotangents(g, info, n, slots, cols=slice(None)):
    blocks = []
    for k in slots:
        block = g[k][:, cols]
        row = lax.broadcasted_iota(jnp.int32, block.shape, 0)
        blocks.append(block * (row < slot_valid(info, n, block.shape[0], k)).astype(F32).astype(BF16))
    return jnp.concatenate(blocks, axis=0)


def delta_kernel(n, rows, info, *refs):
    g, (lse_ref, out_ref, stats_ref), sends = refs[:n], refs[n : n + 3], refs[n + 3 :]
    pairs = lse_ref.shape[0]
    for h in range(pairs):
        do = slot_cotangents(g, info, n, range(n), slice(h * PAIR, (h + 1) * PAIR)).T.astype(F32)
        prod = do * out_ref[h * PAIR : (h + 1) * PAIR]
        stats_ref[h, 0:2] = lse_ref[h]
        for u in range(2):
            part = prod[u * HEAD_DIM : (u + 1) * HEAD_DIM]
            stats_ref[h, 2 + u : 3 + u] = jnp.sum(part, axis=0, keepdims=True)
    for k in range(n):
        sends[k][...] = out_ref[:, k * rows : (k + 1) * rows].astype(BF16)


def merge(lses, deltas):
    top = lses[0]
    for x in lses[1:]:
        top = jnp.maximum(top, x)
    weights = [jnp.exp(x - top) for x in lses]
    total = sum(weights)
    delta = sum(w * d for w, d in zip(weights, deltas)) / total
    return top + jnp.log(total), delta


def backward_kernel(n, rows, info, *refs):
    q, g, stats = refs[:n], refs[n : 2 * n], refs[2 * n : 3 * n]
    top_ref, exp_ref, kt_ref, v_ref = refs[3 * n : 3 * n + 4]
    dk_own, dv_own, d_oth = refs[3 * n + 4 : 3 * n + 7]
    dq = refs[3 * n + 7 :]
    first_pair = pl.program_id(0) * top_ref.shape[0]
    scale = 1.0 / math.sqrt(HEAD_DIM)

    def ordered(j, p, kind, u, slots):
        line = stats[j][p, 2 * kind + u : 2 * kind + u + 1]
        if rows % 128:
            return line[:, slots[0] * rows : (slots[-1] + 1) * rows]
        return jnp.concatenate([line[:, (k ^ j) * rows : ((k ^ j) + 1) * rows] for k in slots], axis=1)

    def run(blocks, rest):
        vs, kt, operands = {}, {}, {}
        pairs = stats[0].shape[0]
        for p in range(pairs):
            lanes = slice(p * PAIR, (p + 1) * PAIR)
            chunks = range(v_ref.shape[1])
            vs[p] = [with_ones(v_ref[first_pair + p, c]) for c in chunks]
            kt[p] = [kt_ref[first_pair + p, c] for c in chunks]
            for b, slots in enumerate(blocks):
                qb = stack_slots(q, slots, lanes) * lane_scale()
                gb = slot_cotangents(g, info, n, slots, lanes)
                gt = gb.T
                cols = slice(slots[0] * rows, (slots[-1] + 1) * rows)
                for u in range(2):
                    lse, delta = merge(
                        [ordered(j, p, 0, u, slots) for j in range(n)], [ordered(j, p, 1, u, slots) for j in range(n)]
                    )
                    operands[p, b, u] = (
                        jnp.exp(top_ref[p, u : u + 1, cols] - lse),
                        jnp.concatenate([head_rows(gt, u), minus_rows(delta)], axis=0),
                        qb * lane_mask(u, 1.0),
                        gb * lane_mask(u, 1.0),
                    )
        count, size = len(vs[0]), vs[0][0].shape[0]
        dks, dvs, dqs = {}, {}, {}

        def add(sums, key, new):
            sums[key] = sums[key] + new if key in sums else new

        def first(item):
            chain, c = item
            return dot(vs[chain[0]][c], operands[chain][1], NN)

        def second(item, dp):
            chain, c = item
            p, b, u = chain
            weight, _, qm, gm = operands[chain]
            block = target_blocks(n, rows).index(blocks[b])
            prob = exp_ref[first_pair + p, 2 * block + u, c].astype(F32) * weight
            ds = (prob * dp).astype(BF16)
            add(dvs, (p, c), dot(prob.astype(BF16), gm, NN))
            add(dks, (p, c), dot(ds, qm, NN))
            add(dqs, chain, dot(kt[p][c][u * HEAD_DIM : (u + 1) * HEAD_DIM], ds, NN))

        def store(p):
            lanes = slice(p * PAIR, (p + 1) * PAIR)
            half = count // 2
            for c in range(half):
                at = slice(c * size, (c + 1) * size)
                dk_own[0, at, lanes] = dks[p, c].astype(BF16)
                dv_own[0, at, lanes] = dvs[p, c].astype(BF16)
                d_oth[0, at, lanes] = dks[p, half + c].astype(BF16)
                d_oth[1, at, lanes] = dvs[p, half + c].astype(BF16)

        chains = [(p, b, u) for p in range(pairs) for b in range(len(blocks)) for u in range(2)]
        items = [(chain, c) for chain in chains for c in range(count)]
        ahead = first(items[0])
        for i, item in enumerate(items):
            now = ahead
            if i + 1 < len(items):
                ahead = first(items[i + 1])
            second(item, now)
            chain, c = item
            if c == count - 1:
                p, b, u = chain
                total = dqs[chain] * scale
                feat = slice(p * PAIR + u * HEAD_DIM, p * PAIR + (u + 1) * HEAD_DIM)
                for j, k in enumerate(blocks[b]):
                    dq[k][feat] = total[:, j * rows : (j + 1) * rows].astype(BF16)
                if i + 1 == len(items) or items[i + 1][0][0] != p:
                    store(p)
        for slots in rest:
            for k in slots:
                dq[k][...] = jnp.zeros_like(dq[k])

    for_valid_blocks(n, rows, info, run)


def context_kernel(n, rows, info, *refs):
    outs, stats, context = refs[:n], refs[n : 2 * n], refs[2 * n]
    lane = lax.broadcasted_iota(jnp.int32, (1, rows), 1)
    valid = (lane < slot_valid(info, n, rows, 0)).astype(F32)
    heads = outs[0].shape[0] // HEAD_DIM
    parts = []
    for head in range(heads):
        feat = slice(head * HEAD_DIM, (head + 1) * HEAD_DIM)
        lses = []
        for j in range(n):
            slot = 0 if rows % 128 else j
            lses.append(stats[j][head // 2, head % 2 : head % 2 + 1, slot * rows : (slot + 1) * rows])
        top = lses[0]
        for x in lses[1:]:
            top = jnp.maximum(top, x)
        weights = [jnp.exp(x - top) for x in lses]
        keep = valid / sum(weights)
        parts.append(sum(outs[j][feat].astype(F32) * (weights[j] * keep) for j in range(n)))
    context[...] = jnp.concatenate(parts, axis=0).T.astype(BF16)


def split_kernel(grad, pieces, sems):
    width = pieces.shape[2]
    copies = [
        pltpu.make_async_copy(grad.at[:, k * width : (k + 1) * width], pieces.at[k], sems.at[k])
        for k in range(pieces.shape[0])
    ]
    for c in copies:
        c.start()
    for c in copies:
        c.wait()


def fill_kernel(info, back, dk_in, dv_in, dk, dv):
    dk[0] = back[0]
    dv[0] = back[1]


def finish_kernel(n, *refs):
    dq, pieces, out, context = refs[:n], refs[n], refs[n + 1], refs[n + 2]
    total = dq[0][...].astype(F32)
    for ref in dq[1:]:
        total = total + ref[...].astype(F32)
    out[...] = total.T.astype(BF16)
    width = pieces.shape[2]
    for k in range(pieces.shape[0]):
        context[:, k * width : (k + 1) * width] = pieces[k]


def compiler_params():
    return pltpu.CompilerParams(vmem_limit_bytes=VMEM_LIMIT)


def stay(x):
    return pltpu.with_memory_space_constraint(x, pltpu.HBM)


def xor_permute(x, axis, size, k):
    return lax.ppermute(x, axis, [(i, i ^ k) for i in range(size)])


def local(queries, keys, values, grad_out, pad_counts):
    rows, width = queries.shape
    src = keys.shape[1]
    n, m = lax.axis_size("seq"), lax.axis_size("head")
    group, seq = lax.axis_index("grp"), lax.axis_index("seq")
    sub = rows // m
    tgt = rows * n
    pairs = width // PAIR
    step = 2 if pairs % 2 == 0 else 1
    sds = jax.ShapeDtypeStruct
    whole = pl.BlockSpec(memory_space=pltpu.VMEM)
    smem = pl.BlockSpec(memory_space=pltpu.SMEM)
    anywhere = pl.BlockSpec(memory_space=pl.ANY)

    info = jnp.concatenate([group[None], seq[None], pad_counts]).astype(jnp.int32)

    def gather(x):
        return [x] + [xor_permute(x, "seq", n, k) for k in range(1, n)]

    def exchange(x):
        return lax.all_to_all(x, "head", split_axis=0, concat_axis=0, tiled=True)

    def plain(kernel, in_specs, out_shape, *args):
        out_specs = jax.tree.map(lambda x: whole, out_shape)
        return pl.pallas_call(
            kernel, in_specs=in_specs, out_specs=out_specs, out_shape=out_shape, compiler_params=compiler_params()
        )(*args)

    def call(kernel, in_specs, out_specs, out_shape, args, flops=0, alias={}):
        return pl.pallas_call(
            kernel,
            grid_spec=pltpu.PrefetchScalarGridSpec(
                num_scalar_prefetch=1, grid=(pairs // step,), in_specs=in_specs, out_specs=out_specs
            ),
            out_shape=out_shape,
            input_output_aliases=alias,
            compiler_params=compiler_params(),
            cost_estimate=pl.CostEstimate(flops=flops, bytes_accessed=1 << 20, transcendentals=0),
        )(info, *args)

    lanes = step * PAIR
    slot_in = [pl.BlockSpec((rows, lanes), lambda h, info: (0, h))] * n
    slot_t = [pl.BlockSpec((lanes, rows), lambda h, info: (h, 0))] * n
    own = pl.BlockSpec((1, src, lanes), lambda h, info: (info[0], 0, h))
    away = pl.BlockSpec((1, src, lanes), lambda h, info: (1 - info[0], 0, h))
    oth = pl.BlockSpec((2, src, lanes), lambda h, info: (0, 0, h))
    lse_spec = pl.BlockSpec((step, 2, tgt), lambda h, info: (h, 0, 0))
    out_spec = pl.BlockSpec((lanes, tgt), lambda h, info: (h, 0))
    stats_spec = pl.BlockSpec((step, 4, tgt), lambda h, info: (h, 0, 0))

    q = gather(queries)
    k_oth, v_oth = xor_permute(keys, "grp", 2, 1), xor_permute(values, "grp", 2, 1)
    pieces = pl.pallas_call(
        split_kernel,
        in_specs=[pl.BlockSpec(memory_space=pltpu.HBM)],
        out_specs=whole,
        out_shape=sds((m, sub, width), BF16),
        scratch_shapes=[pltpu.SemaphoreType.DMA((m,))],
    )(stay(grad_out))
    g = gather(exchange(pieces).reshape(rows, width))

    flop = 24 * tgt * 2 * src * width
    chunk, per = min(256, src), rows * len(target_blocks(n, rows)[0])
    exps = (pairs, 2 * (tgt // per), 2 * src // chunk, chunk, per)
    count = 2 * src // chunk
    lse, top, out_t, exps, kt, v = call(
        lambda *a: forward_kernel(n, rows, *a),
        slot_in + [own] * 4,
        [lse_spec, lse_spec, out_spec, whole, whole, whole],
        [sds((pairs, 2, tgt), F32)] * 2
        + [sds((width, tgt), F32), sds(exps, BF16)]
        + [sds((pairs, count, PAIR, chunk), BF16), sds((pairs, count, chunk, PAIR), BF16)],
        [stay(queries), *q[1:], stay(keys), stay(values), k_oth, v_oth],
        flops=2 * flop,
    )
    stats, *sends = plain(
        lambda *a: delta_kernel(n, rows, *a),
        [smem] + [whole] * (n + 2),
        [sds((pairs, 4, tgt), F32)] + [sds((width, rows), BF16)] * n,
        info, *g, lse, out_t,
    )
    all_stats = gather(stats)
    if rows % 128:

        def reorder(x, j):
            return x.reshape(pairs, 4, n, rows)[:, :, [k ^ j for k in range(n)]].reshape(pairs, 4, tgt)

        all_stats = [all_stats[0]] + [reorder(all_stats[j], j) for j in range(1, n)]
    outs = [sends[0]] + [xor_permute(sends[k], "seq", n, k) for k in range(1, n)]
    grads = call(
        lambda *a: backward_kernel(n, rows, *a),
        slot_in + slot_in + [stats_spec] * n + [lse_spec, whole, whole, whole],
        [own, own, oth] + slot_t,
        [sds((2, src, width), BF16)] * 3 + [sds((width, rows), BF16)] * n,
        [stay(queries), *q[1:], *g, *all_stats, top, exps, kt, v],
        flops=4 * flop,
    )
    (dk, dv, d_oth, *dq), outs = lax.optimization_barrier((grads, outs))
    dq = [dq[0]] + [xor_permute(dq[k], "seq", n, k) for k in range(1, n)]
    back = xor_permute(d_oth, "grp", 2, 1)

    context = plain(
        lambda *a: context_kernel(n, rows, *a),
        [smem] + [whole] * (2 * n),
        sds((rows, width), BF16),
        info, *outs, *all_stats,
    )
    pieces = exchange(context.reshape(m, sub, width))
    grad_keys, grad_values = call(
        fill_kernel,
        [oth, anywhere, anywhere],
        [away] * 2,
        [sds((2, src, width), BF16)] * 2,
        [back, dk, dv],
        alias={2: 0, 3: 1},
    )
    dq, grad_keys, grad_values = lax.optimization_barrier((dq, grad_keys, grad_values))
    grad_queries, context = plain(
        lambda *a: finish_kernel(n, *a),
        [whole] * (n + 1),
        [sds((rows, width), BF16), sds((sub, m * width), BF16)],
        *dq, pieces,
    )
    return (context, grad_queries, grad_keys, grad_values)


def solution(mesh):
    return jax.shard_map(
        local,
        mesh=mesh,
        in_specs=(
            P(("grp", "seq"), "head"),
            P(None, ("grp", "seq"), "head"),
            P(None, ("grp", "seq"), "head"),
            P(("grp", "seq", "head"), None),
            P(),
        ),
        out_specs=(
            P(("grp", "seq", "head"), None),
            P(("grp", "seq"), "head"),
            P(None, ("grp", "seq"), "head"),
            P(None, ("grp", "seq"), "head"),
        ),
        check_vma=False,
    )
```

```python
import math

import jax
import jax.numpy as jnp
from jax import lax
from jax.experimental import pallas as pl
from jax.experimental.pallas import tpu as pltpu
from jax.sharding import PartitionSpec as P

HEAD_DIM = 64
PAIR = 128
LOG2E = math.log2(math.e)
F32 = jnp.float32
BF16 = jnp.bfloat16
VMEM_LIMIT = 16 * 1024 * 1024

NT = (((1,), (1,)), ((), ()))
NN = (((1,), (0,)), ((), ()))


def dot(a, b, dims):
    return lax.dot_general(a, b, dims, preferred_element_type=F32)


def lane_mask(head, value):
    lane = lax.broadcasted_iota(jnp.int32, (1, PAIR), 1)
    return jnp.where((lane // HEAD_DIM) == head, value, 0.0).astype(BF16)


def lane_scale():
    return jnp.full((1, PAIR), 1.0 / math.sqrt(HEAD_DIM), F32).astype(BF16)


def pair_lanes(pair):
    return pl.ds(pl.multiple_of(pair * PAIR, PAIR), PAIR)


def head_features(pair, u):
    return pl.ds(pl.multiple_of(pair * PAIR + u * HEAD_DIM, HEAD_DIM), HEAD_DIM)


def stack_slots(refs, slots, lanes):
    return jnp.concatenate([refs[k][:, lanes] for k in slots], axis=0)


def slot_valid(info, n, rows, k):
    valid = rows * n - info[2 + info[0]]
    return jnp.clip(valid - (info[1] ^ k) * rows, 0, rows)


def any_valid(info, n, rows, slots):
    return sum(slot_valid(info, n, rows, k) for k in slots) > 0


def target_blocks(n, rows):
    per = max(1, min(n, 256 // rows))
    return [list(range(first, min(first + per, n))) for first in range(0, n, per)]


def for_valid_blocks(n, rows, info, run):
    blocks = target_blocks(n, rows)
    some = [any_valid(info, n, rows, slots) for slots in blocks]
    for case in range(1, 1 << len(blocks)):
        chosen = [b for b in range(len(blocks)) if case >> b & 1]
        wanted = True
        for b in range(len(blocks)):
            wanted = jnp.logical_and(wanted, some[b] if b in chosen else jnp.logical_not(some[b]))

        @pl.when(wanted)
        def _(chosen=chosen):
            rest = [blocks[b] for b in range(len(blocks)) if b not in chosen]
            run([blocks[b] for b in chosen], rest)


def chunked(refs):
    rows = min(256, refs[0].shape[0])
    return [x[i * rows : (i + 1) * rows] for x in refs for i in range(x.shape[0] // rows)]


def head_rows(x, u):
    zero = jnp.zeros((HEAD_DIM, x.shape[1]), BF16)
    part = x[u * HEAD_DIM : (u + 1) * HEAD_DIM]
    return jnp.concatenate([part, zero] if u == 0 else [zero, part], axis=0)


def minus_rows(x):
    high = x.astype(BF16).astype(F32)
    mid = (x - high).astype(BF16).astype(F32)
    low = x - high - mid
    row = lax.broadcasted_iota(jnp.int32, (16, x.shape[1]), 0)
    top = jnp.where(row == 0, -high, jnp.where(row == 1, -mid, jnp.where(row == 2, -low, 0.0))).astype(BF16)
    return jnp.concatenate([top, jnp.zeros((PAIR - 16, x.shape[1]), BF16)], axis=0)


def with_ones(x):
    lane = lax.broadcasted_iota(jnp.int32, (x.shape[0], PAIR), 1)
    return jnp.concatenate([x, (lane < 3).astype(F32).astype(BF16)], axis=1)


def forward_kernel(n, rows, info, *refs):
    q = [refs[0], refs[n - 1], *refs[1 : n - 1]]
    k_own, v_own, k_oth, v_oth, lse_ref, top_ref, out_ref, exp_ref, kt_ref, v_ref, q_ref = refs[n:]
    step = k_own.shape[2] // PAIR
    first_pair = pl.program_id(0) * step

    def run(blocks, rest):
        def sources(own, oth, p):
            return chunked([own[0, :, p * PAIR : (p + 1) * PAIR], oth[info[0], :, pair_lanes(first_pair + p)]])

        ks, vts, qts = {}, {}, {}
        for p in range(step):
            lanes = pair_lanes(first_pair + p)
            q_ref[:, lanes] = q[0][:, p * PAIR : (p + 1) * PAIR]
            ks[p] = sources(k_own, k_oth, p)
            vs = sources(v_own, v_oth, p)
            vt = [x.T for x in vs]
            for c in range(len(vs)):
                kt_ref[first_pair + p, c] = ks[p][c].T
                v_ref[first_pair + p, c] = vs[c]
            row = lax.broadcasted_iota(jnp.int32, (16, vt[0].shape[1]), 0)
            ones = (row == 0).astype(F32).astype(BF16)
            for u in range(2):
                vts[p, u] = [jnp.concatenate([x[u * HEAD_DIM : (u + 1) * HEAD_DIM], ones], axis=0) for x in vt]
            for b, slots in enumerate(blocks):
                qts[p, b] = (stack_slots([q_ref, *q[1:]], slots, lanes) * lane_scale()).T

        def scores(chain):
            p, b, u = chain
            qm = head_rows(qts[p, b], u)
            s = [dot(k, qm, NN) for k in ks[p]]
            top = jnp.max(s[0], axis=0, keepdims=True)
            for x in s[1:]:
                top = jnp.maximum(top, jnp.max(x, axis=0, keepdims=True))
            return s, top

        def output(chain, s, top):
            p, b, u = chain
            o = None
            block = target_blocks(n, rows).index(blocks[b])
            for c, (x, v) in enumerate(zip(s, vts[p, u])):
                e = jnp.exp2((x - top) * LOG2E).astype(BF16)
                exp_ref[first_pair + p, 2 * block + u, c] = e
                part = dot(v, e, NN)
                o = part if o is None else o + part
            total = o[HEAD_DIM : HEAD_DIM + 1]
            cols = pl.ds(blocks[b][0] * rows, rows * len(blocks[b]))
            lse_ref[first_pair + p, u : u + 1, cols] = top + jnp.log(total)
            top_ref[first_pair + p, u : u + 1, cols] = top
            out_ref[head_features(first_pair + p, u), cols] = o[:HEAD_DIM] / total

        chains = [(p, b, u) for p in range(step) for b in range(len(blocks)) for u in range(2)]
        ahead = scores(chains[0])
        for i, chain in enumerate(chains):
            now = ahead
            if i + 1 < len(chains):
                ahead = scores(chains[i + 1])
            output(chain, *now)
        for slots in rest:
            width = rows * len(slots)
            cols = pl.ds(slots[0] * rows, width)
            for p in range(step):
                lse_ref[first_pair + p, :, cols] = jnp.zeros((2, width), F32)
                top_ref[first_pair + p, :, cols] = jnp.zeros((2, width), F32)
                out_ref[pair_lanes(first_pair + p), cols] = jnp.zeros((PAIR, width), F32)

    for_valid_blocks(n, rows, info, run)


def slot_cotangents(g, info, n, slots, cols=slice(None)):
    blocks = []
    for k in slots:
        block = g[k][:, cols]
        row = lax.broadcasted_iota(jnp.int32, block.shape, 0)
        blocks.append(block * (row < slot_valid(info, n, block.shape[0], k)).astype(F32).astype(BF16))
    return jnp.concatenate(blocks, axis=0)


def delta_kernel(n, rows, info, *refs):
    g, (lse_ref, out_ref, stats_ref), sends = refs[:n], refs[n : n + 3], refs[n + 3 :]
    pairs = lse_ref.shape[0]
    for h in range(pairs):
        do = slot_cotangents(g, info, n, range(n), slice(h * PAIR, (h + 1) * PAIR)).T.astype(F32)
        prod = do * out_ref[h * PAIR : (h + 1) * PAIR]
        stats_ref[h, 0:2] = lse_ref[h]
        for u in range(2):
            part = prod[u * HEAD_DIM : (u + 1) * HEAD_DIM]
            stats_ref[h, 2 + u : 3 + u] = jnp.sum(part, axis=0, keepdims=True)
    for k in range(n):
        sends[k][...] = out_ref[:, k * rows : (k + 1) * rows].astype(BF16)


def merge(lses, deltas):
    top = lses[0]
    for x in lses[1:]:
        top = jnp.maximum(top, x)
    weights = [jnp.exp(x - top) for x in lses]
    total = sum(weights)
    delta = sum(w * d for w, d in zip(weights, deltas)) / total
    return top + jnp.log(total), delta


def backward_kernel(n, rows, info, *refs):
    q, g, stats = refs[:n], refs[n : 2 * n], refs[2 * n : 3 * n]
    top_ref, exp_ref, kt_ref, v_ref = refs[3 * n : 3 * n + 4]
    dk_own, dv_own, d_oth = refs[3 * n + 4 : 3 * n + 7]
    dq = refs[3 * n + 7 :]
    pairs = dk_own.shape[2] // PAIR
    first_pair = pl.program_id(0) * pairs
    scale = 1.0 / math.sqrt(HEAD_DIM)

    def ordered(j, p, kind, u, slots):
        line = stats[j][first_pair + p, 2 * kind + u : 2 * kind + u + 1]
        if rows % 128:
            return line[:, slots[0] * rows : (slots[-1] + 1) * rows]
        return jnp.concatenate([line[:, (k ^ j) * rows : ((k ^ j) + 1) * rows] for k in slots], axis=1)

    def run(blocks, rest):
        vs, kt, operands = {}, {}, {}
        for p in range(pairs):
            lanes = pair_lanes(first_pair + p)
            chunks = range(v_ref.shape[1])
            vs[p] = [with_ones(v_ref[first_pair + p, c]) for c in chunks]
            kt[p] = [kt_ref[first_pair + p, c] for c in chunks]
            for b, slots in enumerate(blocks):
                qb = stack_slots(q, slots, lanes) * lane_scale()
                gb = slot_cotangents(g, info, n, slots, lanes)
                gt = gb.T
                cols = slice(slots[0] * rows, (slots[-1] + 1) * rows)
                for u in range(2):
                    lse, delta = merge(
                        [ordered(j, p, 0, u, slots) for j in range(n)], [ordered(j, p, 1, u, slots) for j in range(n)]
                    )
                    operands[p, b, u] = (
                        jnp.exp(top_ref[first_pair + p, u : u + 1, cols] - lse),
                        jnp.concatenate([head_rows(gt, u), minus_rows(delta)], axis=0),
                        qb * lane_mask(u, 1.0),
                        gb * lane_mask(u, 1.0),
                    )
        count, size = len(vs[0]), vs[0][0].shape[0]
        dks, dvs, dqs = {}, {}, {}

        def add(sums, key, new):
            sums[key] = sums[key] + new if key in sums else new

        def first(item):
            chain, c = item
            return dot(vs[chain[0]][c], operands[chain][1], NN)

        def second(item, dp):
            chain, c = item
            p, b, u = chain
            weight, _, qm, gm = operands[chain]
            block = target_blocks(n, rows).index(blocks[b])
            prob = exp_ref[first_pair + p, 2 * block + u, c].astype(F32) * weight
            ds = (prob * dp).astype(BF16)
            add(dvs, (p, c), dot(prob.astype(BF16), gm, NN))
            add(dks, (p, c), dot(ds, qm, NN))
            add(dqs, chain, dot(kt[p][c][u * HEAD_DIM : (u + 1) * HEAD_DIM], ds, NN))

        def store(p):
            lanes = slice(p * PAIR, (p + 1) * PAIR)
            half = count // 2
            for c in range(half):
                at = slice(c * size, (c + 1) * size)
                dk_own[0, at, lanes] = dks[p, c].astype(BF16)
                dv_own[0, at, lanes] = dvs[p, c].astype(BF16)
                d_oth[0, at, pair_lanes(first_pair + p)] = dks[p, half + c].astype(BF16)
                d_oth[1, at, pair_lanes(first_pair + p)] = dvs[p, half + c].astype(BF16)

        chains = [(p, b, u) for p in range(pairs) for b in range(len(blocks)) for u in range(2)]
        items = [(chain, c) for chain in chains for c in range(count)]
        ahead = first(items[0])
        for i, item in enumerate(items):
            now = ahead
            if i + 1 < len(items):
                ahead = first(items[i + 1])
            second(item, now)
            chain, c = item
            if c == count - 1:
                p, b, u = chain
                total = dqs[chain] * scale
                for j, k in enumerate(blocks[b]):
                    dq[k][head_features(first_pair + p, u)] = total[:, j * rows : (j + 1) * rows].astype(BF16)
                if i + 1 == len(items) or items[i + 1][0][0] != p:
                    store(p)
        for slots in rest:
            for k in slots:
                for p in range(pairs):
                    dq[k][pair_lanes(first_pair + p)] = jnp.zeros((PAIR, rows), BF16)

    for_valid_blocks(n, rows, info, run)


def context_kernel(n, rows, info, *refs):
    outs, stats, context = refs[:n], refs[n : 2 * n], refs[2 * n]
    lane = lax.broadcasted_iota(jnp.int32, (1, rows), 1)
    valid = (lane < slot_valid(info, n, rows, 0)).astype(F32)
    heads = outs[0].shape[0] // HEAD_DIM
    parts = []
    for head in range(heads):
        feat = slice(head * HEAD_DIM, (head + 1) * HEAD_DIM)
        lses = []
        for j in range(n):
            slot = 0 if rows % 128 else j
            lses.append(stats[j][head // 2, head % 2 : head % 2 + 1, slot * rows : (slot + 1) * rows])
        top = lses[0]
        for x in lses[1:]:
            top = jnp.maximum(top, x)
        weights = [jnp.exp(x - top) for x in lses]
        keep = valid / sum(weights)
        parts.append(sum(outs[j][feat].astype(F32) * (weights[j] * keep) for j in range(n)))
    context[...] = jnp.concatenate(parts, axis=0).T.astype(BF16)


def split_kernel(grad, pieces, sems):
    width = pieces.shape[2]
    copies = [
        pltpu.make_async_copy(grad.at[:, k * width : (k + 1) * width], pieces.at[k], sems.at[k])
        for k in range(pieces.shape[0])
    ]
    for c in copies:
        c.start()
    for c in copies:
        c.wait()


def fill_kernel(info, back, dk_in, dv_in, dk, dv):
    dk[0] = back[0]
    dv[0] = back[1]


def finish_kernel(n, *refs):
    dq, pieces, out, context = refs[:n], refs[n], refs[n + 1], refs[n + 2]
    total = dq[0][...].astype(F32)
    for ref in dq[1:]:
        total = total + ref[...].astype(F32)
    out[...] = total.T.astype(BF16)
    width = pieces.shape[2]
    for k in range(pieces.shape[0]):
        context[:, k * width : (k + 1) * width] = pieces[k]


def compiler_params():
    return pltpu.CompilerParams(vmem_limit_bytes=VMEM_LIMIT)


def stay(x):
    return pltpu.with_memory_space_constraint(x, pltpu.HBM)


def xor_permute(x, axis, size, k):
    return lax.ppermute(x, axis, [(i, i ^ k) for i in range(size)])


def local(queries, keys, values, grad_out, pad_counts):
    rows, width = queries.shape
    src = keys.shape[1]
    n, m = lax.axis_size("seq"), lax.axis_size("head")
    group, seq = lax.axis_index("grp"), lax.axis_index("seq")
    sub = rows // m
    tgt = rows * n
    pairs = width // PAIR
    step = 2 if pairs % 2 == 0 else 1
    sds = jax.ShapeDtypeStruct
    whole = pl.BlockSpec(memory_space=pltpu.VMEM)
    smem = pl.BlockSpec(memory_space=pltpu.SMEM)
    anywhere = pl.BlockSpec(memory_space=pl.ANY)

    info = jnp.concatenate([group[None], seq[None], pad_counts]).astype(jnp.int32)

    def gather(x):
        return [x] + [xor_permute(x, "seq", n, k) for k in range(1, n)]

    def exchange(x):
        return lax.all_to_all(x, "head", split_axis=0, concat_axis=0, tiled=True)

    def plain(kernel, in_specs, out_shape, *args):
        out_specs = jax.tree.map(lambda x: whole, out_shape)
        return pl.pallas_call(
            kernel, in_specs=in_specs, out_specs=out_specs, out_shape=out_shape, compiler_params=compiler_params()
        )(*args)

    def call(kernel, in_specs, out_specs, out_shape, args, flops=0, alias={}):
        return pl.pallas_call(
            kernel,
            grid_spec=pltpu.PrefetchScalarGridSpec(
                num_scalar_prefetch=1, grid=(pairs // step,), in_specs=in_specs, out_specs=out_specs
            ),
            out_shape=out_shape,
            input_output_aliases=alias,
            compiler_params=compiler_params(),
            cost_estimate=pl.CostEstimate(flops=flops, bytes_accessed=1 << 20, transcendentals=0),
        )(info, *args)

    lanes = step * PAIR
    slot_in = pl.BlockSpec((rows, lanes), lambda h, info: (0, h))
    own = pl.BlockSpec((1, src, lanes), lambda h, info: (info[0], 0, h))
    away = pl.BlockSpec((1, src, lanes), lambda h, info: (1 - info[0], 0, h))
    oth = pl.BlockSpec((2, src, lanes), lambda h, info: (0, 0, h))

    q = gather(queries)
    k_oth, v_oth = xor_permute(keys, "grp", 2, 1), xor_permute(values, "grp", 2, 1)
    pieces = pl.pallas_call(
        split_kernel,
        in_specs=[pl.BlockSpec(memory_space=pltpu.HBM)],
        out_specs=whole,
        out_shape=sds((m, sub, width), BF16),
        scratch_shapes=[pltpu.SemaphoreType.DMA((m,))],
    )(stay(grad_out))
    g = gather(exchange(pieces).reshape(rows, width))

    flop = 24 * tgt * 2 * src * width
    chunk, per = min(256, src), rows * len(target_blocks(n, rows)[0])
    exps = (pairs, 2 * (tgt // per), 2 * src // chunk, chunk, per)
    count = 2 * src // chunk
    lse, top, out_t, exps, kt, v, q_own = call(
        lambda *a: forward_kernel(n, rows, *a),
        [slot_in] + [whole] * (n - 1) + [own, own, whole, whole],
        [whole] * 7,
        [sds((pairs, 2, tgt), F32)] * 2
        + [sds((width, tgt), F32), sds(exps, BF16)]
        + [sds((pairs, count, PAIR, chunk), BF16), sds((pairs, count, chunk, PAIR), BF16), sds((rows, width), BF16)],
        [stay(queries), *q[2:], q[1], stay(keys), stay(values), k_oth, v_oth],
        flops=2 * flop,
    )
    stats, *sends = plain(
        lambda *a: delta_kernel(n, rows, *a),
        [smem] + [whole] * (n + 2),
        [sds((pairs, 4, tgt), F32)] + [sds((width, rows), BF16)] * n,
        info, *g, lse, out_t,
    )
    all_stats = gather(stats)
    if rows % 128:

        def reorder(x, j):
            return x.reshape(pairs, 4, n, rows)[:, :, [k ^ j for k in range(n)]].reshape(pairs, 4, tgt)

        all_stats = [all_stats[0]] + [reorder(all_stats[j], j) for j in range(1, n)]
    outs = [sends[0]] + [xor_permute(sends[k], "seq", n, k) for k in range(1, n)]
    grads = call(
        lambda *a: backward_kernel(n, rows, *a),
        [whole] * (3 * n + 4),
        [own, own] + [whole] * (n + 1),
        [sds((2, src, width), BF16)] * 3 + [sds((width, rows), BF16)] * n,
        [q_own, *q[1:], *g, *all_stats, top, exps, kt, v],
        flops=4 * flop,
    )
    (dk, dv, d_oth, *dq), outs = lax.optimization_barrier((grads, outs))
    dq = [dq[0]] + [xor_permute(dq[k], "seq", n, k) for k in range(1, n)]
    back = xor_permute(d_oth, "grp", 2, 1)

    context = plain(
        lambda *a: context_kernel(n, rows, *a),
        [smem] + [whole] * (2 * n),
        sds((rows, width), BF16),
        info, *outs, *all_stats,
    )
    pieces = exchange(context.reshape(m, sub, width))
    grad_keys, grad_values = call(
        fill_kernel,
        [oth, anywhere, anywhere],
        [away] * 2,
        [sds((2, src, width), BF16)] * 2,
        [back, dk, dv],
        alias={2: 0, 3: 1},
    )
    dq, grad_keys, grad_values = lax.optimization_barrier((dq, grad_keys, grad_values))
    grad_queries, context = plain(
        lambda *a: finish_kernel(n, *a),
        [whole] * (n + 1),
        [sds((rows, width), BF16), sds((sub, m * width), BF16)],
        *dq, pieces,
    )
    return (context, grad_queries, grad_keys, grad_values)


def solution(mesh):
    return jax.shard_map(
        local,
        mesh=mesh,
        in_specs=(
            P(("grp", "seq"), "head"),
            P(None, ("grp", "seq"), "head"),
            P(None, ("grp", "seq"), "head"),
            P(("grp", "seq", "head"), None),
            P(),
        ),
        out_specs=(
            P(("grp", "seq", "head"), None),
            P(("grp", "seq"), "head"),
            P(None, ("grp", "seq"), "head"),
            P(None, ("grp", "seq"), "head"),
        ),
        check_vma=False,
    )
```

```python
import math

import jax
import jax.numpy as jnp
from jax import lax
from jax.experimental import pallas as pl
from jax.experimental.pallas import tpu as pltpu
from jax.sharding import PartitionSpec as P

HEAD_DIM = 64
PAIR = 128
LOG2E = math.log2(math.e)
F32 = jnp.float32
BF16 = jnp.bfloat16
VMEM_LIMIT = 16 * 1024 * 1024

NT = (((1,), (1,)), ((), ()))
NN = (((1,), (0,)), ((), ()))


def dot(a, b, dims):
    return lax.dot_general(a, b, dims, preferred_element_type=F32)


def lane_mask(head, value):
    lane = lax.broadcasted_iota(jnp.int32, (1, PAIR), 1)
    return jnp.where((lane // HEAD_DIM) == head, value, 0.0).astype(BF16)


def lane_scale():
    return jnp.full((1, PAIR), 1.0 / math.sqrt(HEAD_DIM), F32).astype(BF16)


def pair_lanes(pair):
    return pl.ds(pl.multiple_of(pair * PAIR, PAIR), PAIR)


def head_features(pair, u):
    return pl.ds(pl.multiple_of(pair * PAIR + u * HEAD_DIM, HEAD_DIM), HEAD_DIM)


def stack_slots(refs, slots, lanes):
    return jnp.concatenate([refs[k][:, lanes] for k in slots], axis=0)


def slot_valid(info, n, rows, k):
    valid = rows * n - info[2 + info[0]]
    return jnp.clip(valid - (info[1] ^ k) * rows, 0, rows)


def any_valid(info, n, rows, slots):
    return sum(slot_valid(info, n, rows, k) for k in slots) > 0


def target_blocks(n, rows):
    per = max(1, min(n, 256 // rows))
    return [list(range(first, min(first + per, n))) for first in range(0, n, per)]


def for_valid_blocks(n, rows, info, run):
    blocks = target_blocks(n, rows)
    some = [any_valid(info, n, rows, slots) for slots in blocks]
    for case in range(1, 1 << len(blocks)):
        chosen = [b for b in range(len(blocks)) if case >> b & 1]
        wanted = True
        for b in range(len(blocks)):
            wanted = jnp.logical_and(wanted, some[b] if b in chosen else jnp.logical_not(some[b]))

        @pl.when(wanted)
        def _(chosen=chosen):
            rest = [blocks[b] for b in range(len(blocks)) if b not in chosen]
            run([blocks[b] for b in chosen], rest)


def chunked(refs):
    rows = min(256, refs[0].shape[0])
    return [x[i * rows : (i + 1) * rows] for x in refs for i in range(x.shape[0] // rows)]


def head_rows(x, u):
    zero = jnp.zeros((HEAD_DIM, x.shape[1]), BF16)
    part = x[u * HEAD_DIM : (u + 1) * HEAD_DIM]
    return jnp.concatenate([part, zero] if u == 0 else [zero, part], axis=0)


def minus_rows(x):
    high = x.astype(BF16).astype(F32)
    mid = (x - high).astype(BF16).astype(F32)
    low = x - high - mid
    row = lax.broadcasted_iota(jnp.int32, (16, x.shape[1]), 0)
    top = jnp.where(row == 0, -high, jnp.where(row == 1, -mid, jnp.where(row == 2, -low, 0.0))).astype(BF16)
    return jnp.concatenate([top, jnp.zeros((PAIR - 16, x.shape[1]), BF16)], axis=0)


def with_ones(x):
    lane = lax.broadcasted_iota(jnp.int32, (x.shape[0], PAIR), 1)
    return jnp.concatenate([x, (lane < 3).astype(F32).astype(BF16)], axis=1)


def forward_kernel(n, rows, info, *refs):
    q = [refs[0], refs[n - 1], *refs[1 : n - 1]]
    k_own, v_own, k_oth, v_oth, lse_ref, top_ref, out_ref, exp_ref, kt_ref, v_ref, q_ref = refs[n:]
    step = k_own.shape[2] // PAIR
    first_pair = pl.program_id(0) * step

    def run(blocks, rest):
        def sources(own, oth, p):
            return chunked([own[0, :, p * PAIR : (p + 1) * PAIR], oth[info[0], :, pair_lanes(first_pair + p)]])

        ks, vts, qts = {}, {}, {}
        for p in range(step):
            lanes = pair_lanes(first_pair + p)
            q_ref[:, lanes] = q[0][:, p * PAIR : (p + 1) * PAIR]
            ks[p] = sources(k_own, k_oth, p)
            vs = sources(v_own, v_oth, p)
            vt = [x.T for x in vs]
            for c in range(len(vs)):
                kt_ref[first_pair + p, c] = ks[p][c].T
                v_ref[first_pair + p, c] = vs[c]
            row = lax.broadcasted_iota(jnp.int32, (16, vt[0].shape[1]), 0)
            ones = (row == 0).astype(F32).astype(BF16)
            for u in range(2):
                vts[p, u] = [jnp.concatenate([x[u * HEAD_DIM : (u + 1) * HEAD_DIM], ones], axis=0) for x in vt]
            for b, slots in enumerate(blocks):
                qts[p, b] = (stack_slots([q_ref, *q[1:]], slots, lanes) * lane_scale()).T

        def scores(chain):
            p, b, u = chain
            qm = head_rows(qts[p, b], u)
            s = [dot(k, qm, NN) for k in ks[p]]
            top = jnp.max(s[0], axis=0, keepdims=True)
            for x in s[1:]:
                top = jnp.maximum(top, jnp.max(x, axis=0, keepdims=True))
            return s, top

        def output(chain, s, top):
            p, b, u = chain
            o = None
            block = target_blocks(n, rows).index(blocks[b])
            for c, (x, v) in enumerate(zip(s, vts[p, u])):
                e = jnp.exp2((x - top) * LOG2E).astype(BF16)
                exp_ref[first_pair + p, 2 * block + u, c] = e
                part = dot(v, e, NN)
                o = part if o is None else o + part
            total = o[HEAD_DIM : HEAD_DIM + 1]
            cols = pl.ds(blocks[b][0] * rows, rows * len(blocks[b]))
            lse_ref[first_pair + p, u : u + 1, cols] = top + jnp.log(total)
            top_ref[first_pair + p, u : u + 1, cols] = top
            out_ref[head_features(first_pair + p, u), cols] = o[:HEAD_DIM] / total

        chains = [(p, b, u) for p in range(step) for b in range(len(blocks)) for u in range(2)]
        ahead = scores(chains[0])
        for i, chain in enumerate(chains):
            now = ahead
            if i + 1 < len(chains):
                ahead = scores(chains[i + 1])
            output(chain, *now)
        for slots in rest:
            width = rows * len(slots)
            cols = pl.ds(slots[0] * rows, width)
            for p in range(step):
                lse_ref[first_pair + p, :, cols] = jnp.zeros((2, width), F32)
                top_ref[first_pair + p, :, cols] = jnp.zeros((2, width), F32)
                out_ref[pair_lanes(first_pair + p), cols] = jnp.zeros((PAIR, width), F32)

    for_valid_blocks(n, rows, info, run)


def slot_cotangents(g, info, n, slots, cols=slice(None)):
    blocks = []
    for k in slots:
        block = g[k][:, cols]
        row = lax.broadcasted_iota(jnp.int32, block.shape, 0)
        blocks.append(block * (row < slot_valid(info, n, block.shape[0], k)).astype(F32).astype(BF16))
    return jnp.concatenate(blocks, axis=0)


def delta_kernel(n, rows, info, *refs):
    g, (lse_ref, out_ref, stats_ref), sends = refs[:n], refs[n : n + 3], refs[n + 3 :]
    pairs = lse_ref.shape[0]
    for h in range(pairs):
        do = slot_cotangents(g, info, n, range(n), slice(h * PAIR, (h + 1) * PAIR)).T.astype(F32)
        prod = do * out_ref[h * PAIR : (h + 1) * PAIR]
        stats_ref[h, 0:2] = lse_ref[h]
        for u in range(2):
            part = prod[u * HEAD_DIM : (u + 1) * HEAD_DIM]
            stats_ref[h, 2 + u : 3 + u] = jnp.sum(part, axis=0, keepdims=True)
    for k in range(n):
        sends[k][...] = out_ref[:, k * rows : (k + 1) * rows].astype(BF16)


def merge(lses, deltas):
    top = lses[0]
    for x in lses[1:]:
        top = jnp.maximum(top, x)
    weights = [jnp.exp(x - top) for x in lses]
    total = sum(weights)
    delta = sum(w * d for w, d in zip(weights, deltas)) / total
    return top + jnp.log(total), delta


def backward_kernel(n, rows, info, *refs):
    q, g, stats = refs[:n], refs[n : 2 * n], refs[2 * n : 3 * n]
    top_ref, exp_ref, kt_ref, v_ref = refs[3 * n : 3 * n + 4]
    dk_own, dv_own, d_oth = refs[3 * n + 4 : 3 * n + 7]
    dq = refs[3 * n + 7 :]
    pairs = dk_own.shape[2] // PAIR
    first_pair = pl.program_id(0) * pairs
    scale = 1.0 / math.sqrt(HEAD_DIM)

    def ordered(j, p, kind, u, slots):
        line = stats[j][first_pair + p, 2 * kind + u : 2 * kind + u + 1]
        if rows % 128:
            return line[:, slots[0] * rows : (slots[-1] + 1) * rows]
        return jnp.concatenate([line[:, (k ^ j) * rows : ((k ^ j) + 1) * rows] for k in slots], axis=1)

    def run(blocks, rest):
        vs, kt, operands = {}, {}, {}
        for p in range(pairs):
            lanes = pair_lanes(first_pair + p)
            chunks = range(v_ref.shape[1])
            vs[p] = [with_ones(v_ref[first_pair + p, c]) for c in chunks]
            kt[p] = [kt_ref[first_pair + p, c] for c in chunks]
            for b, slots in enumerate(blocks):
                qb = stack_slots(q, slots, lanes) * lane_scale()
                gb = slot_cotangents(g, info, n, slots, lanes)
                gt = gb.T
                cols = slice(slots[0] * rows, (slots[-1] + 1) * rows)
                for u in range(2):
                    lse, delta = merge(
                        [ordered(j, p, 0, u, slots) for j in range(n)], [ordered(j, p, 1, u, slots) for j in range(n)]
                    )
                    operands[p, b, u] = (
                        jnp.exp(top_ref[first_pair + p, u : u + 1, cols] - lse),
                        jnp.concatenate([head_rows(gt, u), minus_rows(delta)], axis=0),
                        qb * lane_mask(u, 1.0),
                        gb * lane_mask(u, 1.0),
                    )
        count, size = len(vs[0]), vs[0][0].shape[0]
        dks, dvs, dqs = {}, {}, {}

        def add(sums, key, new):
            sums[key] = sums[key] + new if key in sums else new

        def first(item):
            chain, c = item
            return dot(vs[chain[0]][c], operands[chain][1], NN)

        def second(item, dp):
            chain, c = item
            p, b, u = chain
            weight, _, qm, gm = operands[chain]
            block = target_blocks(n, rows).index(blocks[b])
            prob = exp_ref[first_pair + p, 2 * block + u, c].astype(F32) * weight
            ds = (prob * dp).astype(BF16)
            add(dvs, (p, c), dot(prob.astype(BF16), gm, NN))
            add(dks, (p, c), dot(ds, qm, NN))
            add(dqs, chain, dot(kt[p][c][u * HEAD_DIM : (u + 1) * HEAD_DIM], ds, NN))

        def store(p):
            lanes = slice(p * PAIR, (p + 1) * PAIR)
            half = count // 2
            for c in range(half):
                at = slice(c * size, (c + 1) * size)
                dk_own[0, at, lanes] = dks[p, c].astype(BF16)
                dv_own[0, at, lanes] = dvs[p, c].astype(BF16)
                d_oth[0, at, pair_lanes(first_pair + p)] = dks[p, half + c].astype(BF16)
                d_oth[1, at, pair_lanes(first_pair + p)] = dvs[p, half + c].astype(BF16)

        chains = [(p, b, u) for p in range(pairs) for b in range(len(blocks)) for u in range(2)]
        items = [(chain, c) for chain in chains for c in range(count)]
        ahead = first(items[0])
        for i, item in enumerate(items):
            now = ahead
            if i + 1 < len(items):
                ahead = first(items[i + 1])
            second(item, now)
            chain, c = item
            if c == count - 1:
                p, b, u = chain
                total = dqs[chain] * scale
                for j, k in enumerate(blocks[b]):
                    dq[k][head_features(first_pair + p, u)] = total[:, j * rows : (j + 1) * rows].astype(BF16)
                if i + 1 == len(items) or items[i + 1][0][0] != p:
                    store(p)
        for slots in rest:
            for k in slots:
                for p in range(pairs):
                    dq[k][pair_lanes(first_pair + p)] = jnp.zeros((PAIR, rows), BF16)

    for_valid_blocks(n, rows, info, run)


def context_kernel(n, rows, info, *refs):
    outs, stats, context = refs[:n], refs[n : 2 * n], refs[2 * n]
    lane = lax.broadcasted_iota(jnp.int32, (1, rows), 1)
    valid = (lane < slot_valid(info, n, rows, 0)).astype(F32)
    heads = outs[0].shape[0] // HEAD_DIM
    parts = []
    for head in range(heads):
        feat = slice(head * HEAD_DIM, (head + 1) * HEAD_DIM)
        lses = []
        for j in range(n):
            slot = 0 if rows % 128 else j
            lses.append(stats[j][head // 2, head % 2 : head % 2 + 1, slot * rows : (slot + 1) * rows])
        top = lses[0]
        for x in lses[1:]:
            top = jnp.maximum(top, x)
        weights = [jnp.exp(x - top) for x in lses]
        keep = valid / sum(weights)
        parts.append(sum(outs[j][feat].astype(F32) * (weights[j] * keep) for j in range(n)))
    context[...] = jnp.concatenate(parts, axis=0).T.astype(BF16)


def split_kernel(grad, pieces, sems):
    width = pieces.shape[2]
    copies = [
        pltpu.make_async_copy(grad.at[:, k * width : (k + 1) * width], pieces.at[k], sems.at[k])
        for k in range(pieces.shape[0])
    ]
    for c in copies:
        c.start()
    for c in copies:
        c.wait()


def fill_kernel(info, back, dk_in, dv_in, dk, dv):
    dk[0] = back[0]
    dv[0] = back[1]


def finish_kernel(n, *refs):
    dq, pieces, out, context = refs[:n], refs[n], refs[n + 1], refs[n + 2]
    total = dq[0][...].astype(F32)
    for ref in dq[1:]:
        total = total + ref[...].astype(F32)
    out[...] = total.T.astype(BF16)
    width = pieces.shape[2]
    for k in range(pieces.shape[0]):
        context[:, k * width : (k + 1) * width] = pieces[k]


def compiler_params():
    return pltpu.CompilerParams(vmem_limit_bytes=VMEM_LIMIT)


def stay(x):
    return pltpu.with_memory_space_constraint(x, pltpu.HBM)


def xor_permute(x, axis, size, k):
    return lax.ppermute(x, axis, [(i, i ^ k) for i in range(size)])


def local(queries, keys, values, grad_out, pad_counts):
    rows, width = queries.shape
    src = keys.shape[1]
    n, m = lax.axis_size("seq"), lax.axis_size("head")
    group, seq = lax.axis_index("grp"), lax.axis_index("seq")
    sub = rows // m
    tgt = rows * n
    pairs = width // PAIR
    step = 1
    sds = jax.ShapeDtypeStruct
    whole = pl.BlockSpec(memory_space=pltpu.VMEM)
    smem = pl.BlockSpec(memory_space=pltpu.SMEM)
    anywhere = pl.BlockSpec(memory_space=pl.ANY)

    info = jnp.concatenate([group[None], seq[None], pad_counts]).astype(jnp.int32)

    def gather(x):
        return [x] + [xor_permute(x, "seq", n, k) for k in range(1, n)]

    def exchange(x):
        return lax.all_to_all(x, "head", split_axis=0, concat_axis=0, tiled=True)

    def plain(kernel, in_specs, out_shape, *args):
        out_specs = jax.tree.map(lambda x: whole, out_shape)
        return pl.pallas_call(
            kernel, in_specs=in_specs, out_specs=out_specs, out_shape=out_shape, compiler_params=compiler_params()
        )(*args)

    def call(kernel, in_specs, out_specs, out_shape, args, flops=0, alias={}):
        return pl.pallas_call(
            kernel,
            grid_spec=pltpu.PrefetchScalarGridSpec(
                num_scalar_prefetch=1, grid=(pairs // step,), in_specs=in_specs, out_specs=out_specs
            ),
            out_shape=out_shape,
            input_output_aliases=alias,
            compiler_params=compiler_params(),
            cost_estimate=pl.CostEstimate(flops=flops, bytes_accessed=1 << 20, transcendentals=0),
        )(info, *args)

    lanes = step * PAIR
    slot_in = pl.BlockSpec((rows, lanes), lambda h, info: (0, h))
    own = pl.BlockSpec((1, src, lanes), lambda h, info: (info[0], 0, h))
    away = pl.BlockSpec((1, src, lanes), lambda h, info: (1 - info[0], 0, h))
    oth = pl.BlockSpec((2, src, lanes), lambda h, info: (0, 0, h))

    q = gather(queries)
    k_oth, v_oth = xor_permute(keys, "grp", 2, 1), xor_permute(values, "grp", 2, 1)
    pieces = pl.pallas_call(
        split_kernel,
        in_specs=[pl.BlockSpec(memory_space=pltpu.HBM)],
        out_specs=whole,
        out_shape=sds((m, sub, width), BF16),
        scratch_shapes=[pltpu.SemaphoreType.DMA((m,))],
    )(stay(grad_out))
    g = gather(exchange(pieces).reshape(rows, width))

    flop = 24 * tgt * 2 * src * width
    chunk, per = min(256, src), rows * len(target_blocks(n, rows)[0])
    exps = (pairs, 2 * (tgt // per), 2 * src // chunk, chunk, per)
    count = 2 * src // chunk
    lse, top, out_t, exps, kt, v, q_own = call(
        lambda *a: forward_kernel(n, rows, *a),
        [slot_in] + [whole] * (n - 1) + [own, own, whole, whole],
        [whole] * 7,
        [sds((pairs, 2, tgt), F32)] * 2
        + [sds((width, tgt), F32), sds(exps, BF16)]
        + [sds((pairs, count, PAIR, chunk), BF16), sds((pairs, count, chunk, PAIR), BF16), sds((rows, width), BF16)],
        [stay(queries), *q[2:], q[1], stay(keys), stay(values), k_oth, v_oth],
        flops=2 * flop,
    )
    stats, *sends = plain(
        lambda *a: delta_kernel(n, rows, *a),
        [smem] + [whole] * (n + 2),
        [sds((pairs, 4, tgt), F32)] + [sds((width, rows), BF16)] * n,
        info, *g, lse, out_t,
    )
    all_stats = gather(stats)
    if rows % 128:

        def reorder(x, j):
            return x.reshape(pairs, 4, n, rows)[:, :, [k ^ j for k in range(n)]].reshape(pairs, 4, tgt)

        all_stats = [all_stats[0]] + [reorder(all_stats[j], j) for j in range(1, n)]
    outs = [sends[0]] + [xor_permute(sends[k], "seq", n, k) for k in range(1, n)]
    grads = call(
        lambda *a: backward_kernel(n, rows, *a),
        [whole] * (3 * n + 4),
        [own, own] + [whole] * (n + 1),
        [sds((2, src, width), BF16)] * 3 + [sds((width, rows), BF16)] * n,
        [q_own, *q[1:], *g, *all_stats, top, exps, kt, v],
        flops=4 * flop,
    )
    (dk, dv, d_oth, *dq), outs = lax.optimization_barrier((grads, outs))
    dq = [dq[0]] + [xor_permute(dq[k], "seq", n, k) for k in range(1, n)]
    back = xor_permute(d_oth, "grp", 2, 1)

    context = plain(
        lambda *a: context_kernel(n, rows, *a),
        [smem] + [whole] * (2 * n),
        sds((rows, width), BF16),
        info, *outs, *all_stats,
    )
    pieces = exchange(context.reshape(m, sub, width))
    grad_keys, grad_values = call(
        fill_kernel,
        [oth, anywhere, anywhere],
        [away] * 2,
        [sds((2, src, width), BF16)] * 2,
        [back, dk, dv],
        alias={2: 0, 3: 1},
    )
    dq, grad_keys, grad_values = lax.optimization_barrier((dq, grad_keys, grad_values))
    grad_queries, context = plain(
        lambda *a: finish_kernel(n, *a),
        [whole] * (n + 1),
        [sds((rows, width), BF16), sds((sub, m * width), BF16)],
        *dq, pieces,
    )
    return (context, grad_queries, grad_keys, grad_values)


def solution(mesh):
    return jax.shard_map(
        local,
        mesh=mesh,
        in_specs=(
            P(("grp", "seq"), "head"),
            P(None, ("grp", "seq"), "head"),
            P(None, ("grp", "seq"), "head"),
            P(("grp", "seq", "head"), None),
            P(),
        ),
        out_specs=(
            P(("grp", "seq", "head"), None),
            P(("grp", "seq"), "head"),
            P(None, ("grp", "seq"), "head"),
            P(None, ("grp", "seq"), "head"),
        ),
        check_vma=False,
    )
```
